32 devices in a mesh: groups: 2 (over x), seq: 16 (over z, y, core).
Axes of the slice: x: 2, y: 2, z: 4, core: 2. Of those that a mesh axis runs over, the one named last changes fastest.
Arguments:
- normed: bfloat16 [4096, 8192], P(('groups', 'seq')), parts along dimension 0, may hold values from -8 to 8
- shared_query_rows: bfloat16 [4096, 4096], P(('groups', 'seq')), parts along dimension 0, may hold values from -10 to 10
- shared_key_rows: bfloat16 [4096, 512], P(('groups', 'seq')), parts along dimension 0, may hold values from -4 to 4
- shared_value_rows: bfloat16 [4096, 512], P(('groups', 'seq')), parts along dimension 0, may hold values from -6 to 6
- token_adapter: int32 [4096, 1], P(('groups', 'seq')), parts along dimension 0, may hold values from 0 to 15; in each aligned block of 128 rows (0 to 127, 128 to 255, ...) at most 12 rows name the same one
- adapter_slot_table: int32 [16], replicated, may hold values from 0 to 15, each once
- adapter_down_factors: bfloat16 [16, 8192, 192], P('seq'), may hold values from -0.0625 to 0.0625
- adapter_up_query: bfloat16 [16, 64, 4096], P('seq'), may hold values from -0.375 to 0.375
- adapter_up_key_value: bfloat16 [16, 2, 64, 512], P('seq'), may hold values from -0.375 to 0.375
- token_request: int32 [4096], P('groups'), parts along dimension 0, may hold values from 0 to 3, never falling along the last dimension, each value on 1 to 1024 neighbouring positions
Outputs:
- attention: bfloat16 [4096, 4096], P(('groups', 'seq')), parts along dimension 0
- key_cache: bfloat16 [4096, 512], P(('groups', 'seq')), parts along dimension 0
- value_cache: bfloat16 [4096, 512], P(('groups', 'seq')), parts along dimension 0
The draws below stay inside these ranges and needn't reach their ends.
There are 2 independent parts, one for each index of `groups`. The reference program is written for one: setup_inputs(seed, part) draws one part's arguments, and reference() takes and returns one part's arrays. A program takes and returns all parts, laid end to end along the dimension named above; an argument that names none is the same for every part. Nothing has to cross between parts.
Inputs may be any that keep to these rules, and one draw needn't show every extreme that they name: `token_adapter`: each token names one adapter; among the 128 tokens of one device no adapter is named more than 12 times. `adapter_slot_table`: each slot holds exactly one adapter. `token_request`: request numbers never fall; each request holds 1 to 1024 consecutive tokens.
All inputs are finite; a program needn't handle non-finite values.
Results may differ from the reference program's by a relative error of at most 0.012.
Values may be sent and summed in bfloat16 or wider, within the bound.
No kernel may reach another device: no remote copies, remote signals or barrier semaphores. Data moves between devices by JAX's collectives and lax.ppermute only.
A program may use at most 256 MiB of HBM per device.

```python
import math
import jax
import jax.numpy as jnp
import numpy as np
from jax import lax

MODEL_WIDTH = 8192
QUERY_HEADS = 32
KEY_VALUE_HEADS = 4
HEAD_SIZE = 128
ADAPTER_RANK = 64
TOKENS_PER_INDEX = 128
REQS = 4
SPAN = 8
QUERY_FEATURES = 4096
KEY_VALUE_WIDTH = 512
GROUP_TOKENS = 2048
ADAPTER_COUNT = 16
MOST = 12
PAGE = 8
REQ_MAX = 1024
N_SEQ = 16


def draw_normed(key, part):
    key = jax.random.fold_in(key, 1)
    values = jnp.clip(jax.random.normal(key, (GROUP_TOKENS, MODEL_WIDTH), jnp.float32), -6.0, 6.0)
    return values.astype(jnp.bfloat16)


def draw_shared_query_rows(key, part):
    key = jax.random.fold_in(key, 2)
    values = jnp.clip(jax.random.normal(key, (GROUP_TOKENS, QUERY_HEADS * HEAD_SIZE), jnp.float32), -4.0, 4.0)
    return values.astype(jnp.bfloat16)


def draw_shared_key_rows(key, part):
    key = jax.random.fold_in(key, 3)
    values = jnp.clip(jax.random.normal(key, (GROUP_TOKENS, KEY_VALUE_WIDTH), jnp.float32), -4.0, 4.0)
    return values.astype(jnp.bfloat16)


def steps_of(key, extent, pieces, low, high):
    level, own = 1.0, jax.random.fold_in(key, 6)
    for dim, blocks in pieces:
        steps = jnp.exp(jax.random.uniform(jax.random.fold_in(own, dim), (blocks,), jnp.float32, low / len(pieces), high / len(pieces)))
        level = level * jnp.repeat(steps, extent[dim] // blocks).reshape([-1 if axis == dim else 1 for axis in range(len(extent))])
    return level


def profile(count, total, bound, skew):
    loads = [(1 << 20) // math.isqrt(rank ** skew) + 1 for rank in range(2, count + 1)]
    rest, given = total - bound - (count - 1), [1] * (count - 1)
    while rest > 0:
        movable = [i for i in range(count - 1) if given[i] < bound]
        whole, remaining = sum([loads[i] for i in movable]), rest
        for i in movable:
            extra = min(bound - given[i], max(1, remaining * loads[i] // whole), rest)
            given[i] = given[i] + extra
            rest = rest - extra
    return np.array([bound] + given)


def uneven(own_key, count, total, bound, lean):
    if count == 2:
        one = jax.random.randint(own_key, (), max(1, total - bound), min(bound, total - 1) + 1)
        return jnp.stack([one, total - one])
    lengths = jnp.asarray(profile(count, total, bound, lean), jnp.int32)
    pairs = (count - 1) // 2
    giver, sink = lengths[1:1 + 2 * pairs:2], lengths[2:2 + 2 * pairs:2]
    room = jnp.minimum(giver - 1, bound - sink)
    shifted = jax.random.randint(jax.random.fold_in(own_key, 1), (pairs,), 0, 1 << 20) % (room + 1)
    lengths = lengths.at[1:1 + 2 * pairs:2].set(giver - shifted).at[2:2 + 2 * pairs:2].set(sink + shifted)
    return lengths[jax.random.permutation(jax.random.fold_in(own_key, 2), count)]


def shared_out(rng, own, number, rows, amount, top, reach, skew):
    sequence = jax.random.permutation(rng, amount)
    crowded, usual = load_shares(amount, rows * top, reach, skew, True), load_shares(amount, rows * top, reach, skew, False)
    places = jnp.arange(amount)

    def named(tallies, rotation):
        used = int((tallies > 0).sum())
        fixed = max(1, used // 4)
        moved = fixed + (places - fixed + rotation * (used - fixed)) % max(1, amount - fixed)
        return jnp.zeros((amount,), jnp.int32).at[sequence[jnp.where(places < fixed, places, moved)]].set(jnp.asarray(tallies, jnp.int32))

    tallies = jnp.where(number % 4 == 0, named(crowded, number // 4), named(usual, number - number // 4 - 1))
    mixed = jax.random.permutation(jax.random.fold_in(own, 3), amount)
    donor, taker = mixed[0:amount // 2 * 2:2], mixed[1:amount // 2 * 2:2]
    slack = jnp.minimum(tallies[donor] - 1, reach - tallies[taker]) // 2
    slack = jnp.where((donor == sequence[0]) | (taker == sequence[0]) | (tallies[taker] == 0), 0, jnp.maximum(slack, 0))
    moved = jax.random.randint(jax.random.fold_in(own, 4), (amount // 2,), 0, 1 << 20) % (slack + 1)
    tallies = tallies.at[donor].add(-moved).at[taker].add(moved)
    items = jnp.searchsorted(jnp.cumsum(tallies), jnp.arange(rows * top), side="right").astype(jnp.int32)
    table = items.reshape(top, rows).T
    table = table[jax.random.permutation(jax.random.fold_in(own, 1), rows)]
    rotation = jax.random.randint(jax.random.fold_in(own, 2), (rows, 1), 0, top)
    return jnp.take_along_axis(table, (jnp.arange(top)[None, :] + rotation) % top, axis=1)


def load_shares(count, total, most, lean, full):
    weights = [(1 << 20) // math.isqrt(standing ** lean) + 1 for standing in range(1, count + 1)]
    largest = most if full else min(most, max(-(-total // count), total * weights[0] // sum(weights)))
    least = 1 if total - largest >= count - 1 else 0
    given, spare = [largest] + [least] * (count - 1), total - largest - least * (count - 1)
    while spare > 0:
        free = [i for i in range(1, count) if given[i] < largest] or [i for i in range(1, count) if given[i] < most]
        mass, left = sum([weights[i] for i in free]), spare
        for i in free:
            addition = min(most - given[i], max(1, left * weights[i] // mass), spare)
            given[i] = given[i] + addition
            spare = spare - addition
    return np.array(given)


def noise(key, shape, width, limit, split=(), held_as=jnp.bfloat16):
    values = width * jax.random.normal(key, shape, jnp.float32)
    if split:
        values = values * steps_of(key, shape, split, -0.22, 0.18)
    return jnp.clip(values, -limit, limit).astype(held_as)


def setup_inputs(seed: int = 0, part: int = 0) -> dict:
    key_list = jax.random.split(jax.random.key(seed), 11)
    part_splits = jax.random.split(jax.random.fold_in(key_list[10], part), 11)
    normed = draw_normed(jax.random.fold_in(jax.random.fold_in(key_list[10], part), 71), part)
    shared_query_rows = draw_shared_query_rows(jax.random.fold_in(jax.random.fold_in(key_list[10], part), 71), part)
    shared_key_rows = draw_shared_key_rows(jax.random.fold_in(jax.random.fold_in(key_list[10], part), 71), part)
    shared_value_rows = noise(part_splits[3], (GROUP_TOKENS, KEY_VALUE_WIDTH), 1.0, 6.0, ((0, 16),))
    token_adapter_keys = jax.random.split(jax.random.fold_in(part_splits[4], 1), GROUP_TOKENS // TOKENS_PER_INDEX)
    token_adapter_turns = jax.random.permutation(jax.random.fold_in(part_splits[4], 3), GROUP_TOKENS // TOKENS_PER_INDEX)
    token_adapter = jax.vmap(lambda own, number: shared_out(jax.random.fold_in(part_splits[4], 2), own, number, TOKENS_PER_INDEX, ADAPTER_COUNT, 1, MOST, 2))(token_adapter_keys, token_adapter_turns).reshape((GROUP_TOKENS, 1))
    adapter_slot_table = jax.random.permutation(key_list[5], ADAPTER_COUNT).astype(jnp.int32)
    adapter_down_factors = noise(key_list[6], (ADAPTER_COUNT, MODEL_WIDTH, 3 * ADAPTER_RANK), MODEL_WIDTH ** -0.5, 0.0625, ((0, 16),))
    adapter_up_query = noise(key_list[7], (ADAPTER_COUNT, ADAPTER_RANK, QUERY_FEATURES), (4 * ADAPTER_RANK) ** -0.5, 0.375, ((0, 16),))
    adapter_up_key_value = noise(key_list[8], (ADAPTER_COUNT, 2, ADAPTER_RANK, KEY_VALUE_WIDTH), (4 * ADAPTER_RANK) ** -0.5, 0.375, ((0, 16),))
    token_request = jnp.searchsorted(jnp.cumsum(uneven(part_splits[9], REQS, GROUP_TOKENS, REQ_MAX, 2)), jnp.arange(GROUP_TOKENS), side="right").astype(jnp.int32)
    return dict(normed=normed, shared_query_rows=shared_query_rows, shared_key_rows=shared_key_rows, shared_value_rows=shared_value_rows, token_adapter=token_adapter, adapter_slot_table=adapter_slot_table, adapter_down_factors=adapter_down_factors, adapter_up_query=adapter_up_query, adapter_up_key_value=adapter_up_key_value, token_request=token_request)


def reference(normed, shared_query_rows, shared_key_rows, shared_value_rows, token_adapter, adapter_slot_table, adapter_down_factors, adapter_up_query, adapter_up_key_value, token_request):
    query_width = shared_query_rows.shape[1]
    kv_width = shared_key_rows.shape[1]
    slot_token = lax.optimization_barrier(jnp.sum(jnp.where(token_adapter[:, 0][:, None] == jnp.arange(ADAPTER_COUNT, dtype=jnp.int32)[None, :], adapter_slot_table[None, :], 0), axis=1)).astype(jnp.int32)
    ordering = jnp.argsort(slot_token, stable=True).astype(jnp.int32)
    counts = lax.optimization_barrier(jnp.sum((slot_token[:, None] == jnp.arange(ADAPTER_COUNT, dtype=jnp.int32)[None, :]).astype(jnp.int32), axis=0))
    starts = (jnp.cumsum(counts) - counts).astype(jnp.int32)
    capacity = MOST * N_SEQ
    ordering_padded = jnp.concatenate([ordering, jnp.zeros((capacity,), jnp.int32)])
    out_width = query_width + 2 * kv_width

    def per_slot(delta, store_slot_index):
        row_position = lax.dynamic_slice(ordering_padded, (starts[store_slot_index],), (capacity,))
        is_live = jnp.arange(capacity) < counts[store_slot_index]
        down_projected = jnp.dot(normed[row_position], adapter_down_factors[store_slot_index], preferred_element_type=jnp.float32).astype(jnp.bfloat16)
        adapter_query_update = jnp.dot(down_projected[:, :ADAPTER_RANK], adapter_up_query[store_slot_index], preferred_element_type=jnp.float32).astype(jnp.bfloat16)
        adapter_key_update = jnp.dot(down_projected[:, ADAPTER_RANK:2 * ADAPTER_RANK], adapter_up_key_value[store_slot_index, 0], preferred_element_type=jnp.float32).astype(jnp.bfloat16)
        adapter_value_update = jnp.dot(down_projected[:, 2 * ADAPTER_RANK:], adapter_up_key_value[store_slot_index, 1], preferred_element_type=jnp.float32).astype(jnp.bfloat16)
        joined = jnp.concatenate([adapter_query_update, adapter_key_update, adapter_value_update], axis=1)
        target = jnp.where(is_live, row_position, GROUP_TOKENS).astype(jnp.int32)
        return (delta.at[target].set(joined, mode='drop'), None)
    delta, _ = lax.scan(per_slot, jnp.zeros((GROUP_TOKENS, out_width), jnp.bfloat16), jnp.arange(ADAPTER_COUNT, dtype=jnp.int32))
    query_rows = (shared_query_rows.astype(jnp.float32) + delta[:, :query_width].astype(jnp.float32)).astype(jnp.bfloat16)
    gathered_keys = (shared_key_rows.astype(jnp.float32) + delta[:, query_width:query_width + kv_width].astype(jnp.float32)).astype(jnp.bfloat16)
    gathered_values = (shared_value_rows.astype(jnp.float32) + delta[:, query_width + kv_width:].astype(jnp.float32)).astype(jnp.bfloat16)
    key_cache = gathered_keys.reshape(N_SEQ, N_SEQ, PAGE, kv_width).transpose(1, 0, 2, 3).reshape(GROUP_TOKENS, kv_width)
    value_cache = gathered_values.reshape(N_SEQ, N_SEQ, PAGE, kv_width).transpose(1, 0, 2, 3).reshape(GROUP_TOKENS, kv_width)
    token_group = QUERY_HEADS // KEY_VALUE_HEADS
    request_span_rows = (SPAN + 1) * TOKENS_PER_INDEX
    keys_extended = jnp.concatenate([jnp.zeros((SPAN * TOKENS_PER_INDEX, kv_width), gathered_keys.dtype), gathered_keys], axis=0)
    values_extended = jnp.concatenate([jnp.zeros((SPAN * TOKENS_PER_INDEX, kv_width), gathered_values.dtype), gathered_values], axis=0)
    ids_padded = jnp.concatenate([jnp.full((SPAN * TOKENS_PER_INDEX,), -1, jnp.int32), token_request])

    def block(device):
        span_first = (device * TOKENS_PER_INDEX).astype(jnp.int32)
        query_tile_rows = lax.dynamic_slice_in_dim(query_rows, span_first, TOKENS_PER_INDEX, 0).reshape(TOKENS_PER_INDEX, KEY_VALUE_HEADS, token_group, HEAD_SIZE).astype(jnp.float32)
        key_tile_rows = lax.dynamic_slice_in_dim(keys_extended, span_first, request_span_rows, 0).reshape(request_span_rows, KEY_VALUE_HEADS, HEAD_SIZE).astype(jnp.float32)
        value_tile_rows = lax.dynamic_slice_in_dim(values_extended, span_first, request_span_rows, 0).reshape(request_span_rows, KEY_VALUE_HEADS, HEAD_SIZE).astype(jnp.float32)
        query_ids = lax.dynamic_slice_in_dim(token_request, span_first, TOKENS_PER_INDEX, 0)
        key_ids = lax.dynamic_slice_in_dim(ids_padded, span_first, request_span_rows, 0)
        offsets = jnp.arange(request_span_rows) - SPAN * TOKENS_PER_INDEX
        allowed = (key_ids[None, :] == query_ids[:, None]) & (offsets[None, :] <= jnp.arange(TOKENS_PER_INDEX)[:, None])
        scores = jnp.einsum('tgjd,sgd->gjts', query_tile_rows, key_tile_rows) / math.sqrt(HEAD_SIZE)
        scores = jnp.where(allowed[None, None], scores, -1e+30)
        largest = lax.optimization_barrier(jnp.max(scores, axis=-1, keepdims=True))
        raised = jnp.exp(scores - largest)
        weights = (raised / lax.optimization_barrier(jnp.sum(raised, axis=-1, keepdims=True))).astype(jnp.bfloat16)
        weights = lax.optimization_barrier(weights).astype(jnp.float32)
        blended = jnp.einsum('gjts,sgd->tgjd', weights, value_tile_rows)
        return blended.reshape(TOKENS_PER_INDEX, query_width).astype(jnp.bfloat16)
    attention = lax.map(block, jnp.arange(N_SEQ, dtype=jnp.int32)).reshape(GROUP_TOKENS, query_width)
    return (attention, key_cache, value_cache)
```

```python
import functools
import math

import jax
import jax.numpy as jnp
from jax import lax
from jax.experimental import pallas as pl
from jax.experimental.pallas import tpu as pltpu
from jax.sharding import PartitionSpec as P

KEY_VALUE_HEADS = 4
HEAD_SIZE = 128
SUBLANES = 8
PLANE = 4
VMEM_BYTES = 48 * 1024 * 1024


def params(**kw):
    return pltpu.CompilerParams(vmem_limit_bytes=VMEM_BYTES, **kw)


def f32_dot(a, b):
    return jnp.dot(a, b, preferred_element_type=jnp.float32)


def lane_iota(shape):
    return lax.broadcasted_iota(jnp.int32, shape, 1)


def row_iota(shape):
    return lax.broadcasted_iota(jnp.int32, shape, 0)


def place_tokens(adapter, table_ref, stores):
    count = adapter.shape[0]
    rows, lanes = row_iota((count, count)), lane_iota((count, count))
    as_row = jnp.sum(jnp.where(rows == lanes, adapter, 0.0), axis=0, keepdims=True)
    same = adapter == as_row
    place_col = jnp.sum(jnp.where(same & (lanes < rows), 1.0, 0.0), axis=1, keepdims=True)
    place_row = jnp.sum(jnp.where(same & (rows < lanes), 1.0, 0.0), axis=0, keepdims=True)

    def owner(ids):
        result = jnp.zeros_like(ids)
        for k in range(stores):
            result = jnp.where(ids == float(k), table_ref[k].astype(jnp.float32), result)
        return result

    out = []
    for ids, place in ((adapter, place_col), (as_row, place_row)):
        block = jnp.floor(place * (1.0 / SUBLANES))
        out.append((owner(ids) * SUBLANES + place - block * SUBLANES, block))
    return out


def dispatch_kernel(full, fold, per_width, stores, adapter_ref, table_ref, a_ref, b_ref, x_ref, ids_ref, row_scr):
    step = pl.program_id(0)
    tokens = adapter_ref.shape[0]
    rows = x_ref.shape[0]

    @pl.when(step == 0)
    def _():
        cols, lanes = place_tokens(adapter_ref[...].astype(jnp.float32), table_ref, stores)
        lane = lane_iota((tokens, 128))
        ids_ref[...] = jnp.where(lane == 0, cols[0], jnp.where(lane == 1, cols[1], 0.0)).astype(jnp.int32)
        row_scr[0:1, :] = lanes[0]
        row_scr[1:2, :] = lanes[1]

    at = row_scr[0:1, :].astype(jnp.int32)
    block = row_scr[1:2, :].astype(jnp.int32)
    target = row_iota((rows, tokens))

    if full:

        @pl.when(step < full * per_width)
        def _():
            pick = ((at == target) & (block == step // per_width)).astype(jnp.bfloat16)
            x_ref[...] = f32_dot(pick, a_ref[...]).astype(jnp.bfloat16)

    if fold:

        @pl.when(step >= full * per_width)
        def _():
            low = ((at == target) & (block == full)).astype(jnp.bfloat16)
            high = ((at + 4 == target) & (block == full)).astype(jnp.bfloat16)
            x_ref[...] = (f32_dot(low, a_ref[...]) + f32_dot(high, b_ref[...])).astype(jnp.bfloat16)


def dispatch(normed, token_adapter, table, full, fold):
    tokens, width = normed.shape
    stores = table.shape[0]
    column = width // 4
    per_width, half = width // column, width // 2 // column
    steps = full * per_width + fold * half

    def a_map(i):
        return (0, jnp.where(i < full * per_width, i % per_width, i - full * per_width))

    def b_map(i):
        return (0, jnp.where(i < full * per_width, half, i - full * per_width + half))

    return pl.pallas_call(
        functools.partial(dispatch_kernel, full, fold, per_width, stores),
        grid=(steps,),
        in_specs=[
            pl.BlockSpec((tokens, 1), lambda i: (0, 0)),
            pl.BlockSpec(memory_space=pltpu.SMEM),
            pl.BlockSpec((tokens, column), a_map),
            pl.BlockSpec((tokens, column), b_map),
        ],
        out_specs=[
            pl.BlockSpec((stores * SUBLANES, column), lambda i: (0, i)),
            pl.BlockSpec((tokens, 128), lambda i: (0, 0)),
        ],
        out_shape=[
            jax.ShapeDtypeStruct((stores * SUBLANES, steps * column), jnp.bfloat16),
            jax.ShapeDtypeStruct((tokens, 128), jnp.int32),
        ],
        scratch_shapes=[pltpu.VMEM((8, tokens), jnp.float32)],
        compiler_params=params(),
        name="dispatch",
    )(token_adapter, table, normed, normed)


def project_kernel(full, fold, steps, *refs):
    refs = list(refs)
    low_refs = [(refs.pop(0), refs.pop(0)) for _ in range(full)]
    fold_ref = refs.pop(0) if fold else None
    down_low, down_high, up_query, up_kv, dkv_ref, dq_ref, acc = refs
    step = pl.program_id(0)
    rank = up_query.shape[1]

    @pl.when(step == 0)
    def _():
        acc[...] = jnp.zeros_like(acc)

    low, high = down_low[0], down_high[0]
    for b, (x_low, x_high) in enumerate(low_refs):
        acc[b] += f32_dot(x_low[...], low) + f32_dot(x_high[...], high)
    if fold:
        acc[full] += f32_dot(fold_ref[...], low)
        acc[full + 1] += f32_dot(fold_ref[...], high)

    @pl.when(step == steps - 1)
    def _():
        kv_width, query_width = up_kv.shape[3], up_query.shape[2]
        for b in range(full):
            shrunk = acc[b].astype(jnp.bfloat16)
            at = b * 2 * kv_width
            for i in range(2):
                piece = shrunk[:, (i + 1) * rank : (i + 2) * rank]
                dkv_ref[:, at + i * kv_width : at + (i + 1) * kv_width] = f32_dot(piece, up_kv[0, i]).astype(jnp.bfloat16)
            dq_ref[:, b * query_width : (b + 1) * query_width] = f32_dot(shrunk[:, :rank], up_query[0]).astype(jnp.bfloat16)
        if fold:
            rows = acc.shape[1]
            upper = (row_iota((rows, 1)) % SUBLANES) >= 4
            mixed = jnp.where(upper, acc[full + 1], acc[full]).reshape(rows // SUBLANES, SUBLANES, 3 * rank)
            both = mixed + jnp.concatenate([mixed[:, 4:], mixed[:, :4]], axis=1)
            shrunk = both.reshape(rows, 3 * rank).astype(jnp.bfloat16)
            delta = [f32_dot(shrunk[:, (i + 1) * rank : (i + 2) * rank], up_kv[0, i]) for i in range(2)]
            dkv_ref[:, full * 2 * kv_width :] = jnp.where(upper, delta[1], delta[0]).astype(jnp.bfloat16)
            half = query_width // 2
            piece = shrunk[:, :rank]
            delta = [f32_dot(piece, up_query[0, :, i * half : (i + 1) * half]) for i in range(2)]
            dq_ref[:, full * query_width :] = jnp.where(upper, delta[1], delta[0]).astype(jnp.bfloat16)


def project(x, down, up_query, up_kv, full, fold):
    rows = x.shape[0]
    _, width, ranks = down.shape
    column = width // 8
    steps = width // 2 // column
    query_width, kv_width = up_query.shape[2], up_kv.shape[3]
    in_specs = []
    for b in range(full):
        in_specs.append(pl.BlockSpec((rows, column), lambda i, b=b: (0, 2 * b * steps + i)))
        in_specs.append(pl.BlockSpec((rows, column), lambda i, b=b: (0, (2 * b + 1) * steps + i)))
    if fold:
        in_specs.append(pl.BlockSpec((rows, column), lambda i: (0, 2 * full * steps + i)))
    blocks = len(in_specs)
    in_specs += [
        pl.BlockSpec((1, column, ranks), lambda i: (0, i, 0)),
        pl.BlockSpec((1, column, ranks), lambda i: (0, steps + i, 0)),
        pl.BlockSpec(up_query.shape, lambda i: (0, 0, 0)),
        pl.BlockSpec(up_kv.shape, lambda i: (0, 0, 0, 0)),
    ]
    shapes = [
        (rows, (2 * full + fold) * kv_width),
        (rows, full * query_width + fold * query_width // 2),
    ]
    return pl.pallas_call(
        functools.partial(project_kernel, full, fold, steps),
        grid=(steps,),
        in_specs=in_specs,
        out_specs=[pl.BlockSpec(s, lambda i: (0, 0)) for s in shapes],
        out_shape=[jax.ShapeDtypeStruct(s, jnp.bfloat16) for s in shapes],
        scratch_shapes=[pltpu.VMEM((full + 2 * fold, rows, ranks), jnp.float32)],
        compiler_params=params(),
        name="project",
    )(*([x] * blocks), down, down, up_query, up_kv)


def picks(ids, rows, block, shift):
    at, blocks = ids[:, 0:1], ids[:, 1:2]
    return ((at + shift == lane_iota((ids.shape[0], rows))) & (blocks == block)).astype(jnp.bfloat16)


def correct_kernel(full, fold, ids_ref, dkv_ref, sk_ref, sv_ref, k_ref, v_ref, kv_ref):
    rows = dkv_ref.shape[0]
    width = sk_ref.shape[1]
    ids = ids_ref[...]
    total = [None, None]
    for i in range(2):
        for b in range(full):
            at = (2 * b + i) * width
            term = f32_dot(picks(ids, rows, b, 0), dkv_ref[:, at : at + width])
            total[i] = term if total[i] is None else total[i] + term
        if fold:
            term = f32_dot(picks(ids, rows, full, 4 * i), dkv_ref[:, 2 * full * width :])
            total[i] = term if total[i] is None else total[i] + term
    keys = (sk_ref[...].astype(jnp.float32) + total[0]).astype(jnp.bfloat16)
    values = (sv_ref[...].astype(jnp.float32) + total[1]).astype(jnp.bfloat16)
    k_ref[...] = keys
    v_ref[...] = values
    kv_ref[:, :width] = keys
    kv_ref[:, width:] = values


def correct(ids, dkv, shared_keys, shared_values, full, fold):
    rows, width = shared_keys.shape
    one = jax.ShapeDtypeStruct((rows, width), jnp.bfloat16)
    return pl.pallas_call(
        functools.partial(correct_kernel, full, fold),
        out_shape=[one, one, jax.ShapeDtypeStruct((rows, 2 * width), jnp.bfloat16)],
        compiler_params=params(),
        name="correct",
    )(ids, dkv, shared_keys, shared_values)


def window_chunks(kv, devices, reach):
    planes = reach // PLANE
    chunks = [(0, 0, kv)]
    for back in range(1, planes + 1):
        hop = back * PLANE
        chunks.append((back, 0, lax.ppermute(kv, "seq", [(i, i + hop) for i in range(devices - hop)])))
    bit = PLANE // 2
    while bit:
        swap = [(i, i ^ bit) for i in range(devices)]
        chunks = chunks + [(back, mark ^ bit, lax.ppermute(rows, "seq", swap)) for back, mark, rows in chunks]
        bit //= 2
    return chunks


def attend_kernel(full, fold, reach, tags, *refs):
    refs = list(refs)
    me_ref, ids_ref, request_ref, sq_ref = (refs.pop(0) for _ in range(4))
    dq_refs = [refs.pop(0) for _ in range(full + fold)]
    chunk_refs = [(refs.pop(0), refs.pop(0)) for _ in tags]
    out_ref, bias, keys, values, query = refs
    head = pl.program_id(0)
    me = me_ref[0]
    tokens = sq_ref.shape[0]
    here = reach * tokens

    @pl.when(head == 0)
    def _():
        rows, lanes = row_iota((tokens, tokens)), lane_iota((tokens, tokens))
        own = request_ref[pl.ds(me, 1), :].astype(jnp.float32)
        own = jnp.sum(jnp.where(rows == lanes, own, 0.0), axis=1, keepdims=True)
        for at in range(reach + 1):
            source = me - reach + at
            theirs = request_ref[pl.ds(jnp.maximum(source, 0), 1), :].astype(jnp.float32)
            theirs = jnp.where(source >= 0, theirs, -1.0)
            allowed = own == theirs
            if at == reach:
                allowed = allowed & (lanes <= rows)
            bias[:, at * tokens : (at + 1) * tokens] = jnp.where(allowed, 0.0, -1e30)

    zeros = jnp.zeros((tokens, HEAD_SIZE), jnp.bfloat16)
    for at in range(reach):

        @pl.when(me - reach + at < 0)
        def _(at=at):
            keys[at * tokens : (at + 1) * tokens, :] = zeros
            values[at * tokens : (at + 1) * tokens, :] = zeros

    for (back, mark), (k_ref, v_ref) in zip(tags, chunk_refs):
        source = (me // PLANE - back) * PLANE + jnp.bitwise_xor(me % PLANE, mark)
        at = source - me + reach

        @pl.when((source >= 0) & (at >= 0) & (at <= reach))
        def _(at=at, k_ref=k_ref, v_ref=v_ref):
            place = pl.ds(pl.multiple_of(at * tokens, tokens), tokens)
            keys[place, :] = k_ref[...]
            values[place, :] = v_ref[...]

    ids = ids_ref[...]
    slots = dq_refs[0].shape[0]
    delta = sq_ref[...].astype(jnp.float32)
    correction = None
    for b in range(full):
        term = f32_dot(picks(ids, slots, b, 0), dq_refs[b][...])
        correction = term if correction is None else correction + term
    if fold:
        shift = 4 * (head // (KEY_VALUE_HEADS // 2))
        term = f32_dot(picks(ids, slots, full, shift), dq_refs[full][...])
        correction = term if correction is None else correction + term
    query[...] = (delta + correction).astype(jnp.bfloat16)

    scale = 1.0 / math.sqrt(HEAD_SIZE)
    for j in range(sq_ref.shape[1] // HEAD_SIZE):
        span = slice(j * HEAD_SIZE, (j + 1) * HEAD_SIZE)
        scores = lax.dot_general(
            query[:, span], keys[...], (((1,), (1,)), ((), ())), preferred_element_type=jnp.float32
        )
        scores = scores * scale + bias[...]
        raised = jnp.exp(scores - jnp.max(scores, axis=1, keepdims=True))
        total = jnp.sum(raised, axis=1, keepdims=True)
        blended = f32_dot(raised.astype(jnp.bfloat16), values[...])
        out_ref[:, span] = (blended / total).astype(jnp.bfloat16)


def attend(me, ids, requests, shared_query, dq, chunks, full, fold, reach):
    tokens, query_width = shared_query.shape
    slots = dq.shape[0]
    block = query_width // KEY_VALUE_HEADS
    in_specs = [
        pl.BlockSpec(memory_space=pltpu.SMEM),
        pl.BlockSpec(ids.shape, lambda g: (0, 0)),
        pl.BlockSpec(requests.shape, lambda g: (0, 0)),
        pl.BlockSpec((tokens, block), lambda g: (0, g)),
    ]
    for b in range(full):
        in_specs.append(pl.BlockSpec((slots, block), lambda g, b=b: (0, b * KEY_VALUE_HEADS + g)))
    if fold:
        in_specs.append(
            pl.BlockSpec((slots, block), lambda g: (0, full * KEY_VALUE_HEADS + g % (KEY_VALUE_HEADS // 2)))
        )
    operands = [me, ids, requests, shared_query] + [dq] * (full + fold)
    for _, _, rows in chunks:
        in_specs.append(pl.BlockSpec((tokens, HEAD_SIZE), lambda g: (0, g)))
        in_specs.append(pl.BlockSpec((tokens, HEAD_SIZE), lambda g: (0, KEY_VALUE_HEADS + g)))
        operands += [rows, rows]
    window = (reach + 1) * tokens
    return pl.pallas_call(
        functools.partial(attend_kernel, full, fold, reach, tuple((b, m) for b, m, _ in chunks)),
        grid=(KEY_VALUE_HEADS,),
        in_specs=in_specs,
        out_specs=pl.BlockSpec((tokens, block), lambda g: (0, g)),
        out_shape=jax.ShapeDtypeStruct((tokens, query_width), jnp.bfloat16),
        scratch_shapes=[
            pltpu.VMEM((tokens, window), jnp.float32),
            pltpu.VMEM((window, HEAD_SIZE), jnp.bfloat16),
            pltpu.VMEM((window, HEAD_SIZE), jnp.bfloat16),
            pltpu.VMEM((tokens, block), jnp.bfloat16),
        ],
        compiler_params=params(),
        name="attend",
    )(*operands)


def exchange(rows, devices):
    width = rows.shape[1]
    out = lax.all_to_all(
        rows.reshape(devices, rows.shape[0] // devices, width), "seq", split_axis=0, concat_axis=0, tiled=True
    )
    return out.reshape(rows.shape)


def local(
    normed,
    shared_query_rows,
    shared_key_rows,
    shared_value_rows,
    token_adapter,
    adapter_slot_table,
    adapter_down_factors,
    adapter_up_query,
    adapter_up_key_value,
    token_request,
):
    tokens = normed.shape[0]
    devices = lax.axis_size("seq")
    reach = devices // 2
    most = max(2, 3 * tokens // (2 * devices))
    fours = -(-most // 4)
    full, fold = fours // 2, fours % 2

    outgoing, ids = dispatch(normed, token_adapter, adapter_slot_table, full, fold)
    incoming = exchange(outgoing, devices)
    dkv, dq = project(incoming, adapter_down_factors, adapter_up_query, adapter_up_key_value, full, fold)
    dkv = exchange(dkv, devices)
    keys, values, kv = correct(ids, dkv, shared_key_rows, shared_value_rows, full, fold)
    dq = exchange(dq, devices)
    chunks = window_chunks(kv, devices, reach)
    key_cache = exchange(keys, devices)
    value_cache = exchange(values, devices)
    me = lax.axis_index("seq").astype(jnp.int32).reshape(1)
    attention = attend(
        me, ids, token_request.reshape(devices, tokens), shared_query_rows, dq, chunks, full, fold, reach
    )
    return (attention, key_cache, value_cache)


def solution(mesh):
    rows = P(("groups", "seq"), None)
    return jax.shard_map(
        local,
        mesh=mesh,
        in_specs=(
            rows,
            rows,
            rows,
            rows,
            rows,
            P(),
            P("seq", None, None),
            P("seq", None, None),
            P("seq", None, None, None),
            P("groups"),
        ),
        out_specs=(rows, rows, rows),
        check_vma=False,
    )
```

```python
import functools
import math

import jax
import jax.numpy as jnp
from jax import lax
from jax.experimental import pallas as pl
from jax.experimental.pallas import tpu as pltpu
from jax.sharding import PartitionSpec as P

KEY_VALUE_HEADS = 4
HEAD_SIZE = 128
SUBLANES = 8
PLANE = 4
MIB = 1024 * 1024


def params(mib=40):
    return pltpu.CompilerParams(vmem_limit_bytes=mib * MIB)


def cost(flops, moved):
    return pl.CostEstimate(flops=flops, bytes_accessed=moved, transcendentals=0)


def f32_dot(a, b):
    return jnp.dot(a, b, preferred_element_type=jnp.float32)


def lane_iota(shape):
    return lax.broadcasted_iota(jnp.int32, shape, 1)


def row_iota(shape):
    return lax.broadcasted_iota(jnp.int32, shape, 0)


def place_tokens(as_row, table_ref, stores):
    count = as_row.shape[1]
    rows, lanes = row_iota((count, count)), lane_iota((count, count))
    adapter = jnp.sum(jnp.where(rows == lanes, as_row, 0.0), axis=1, keepdims=True)
    same = adapter == as_row
    place_col = jnp.sum(jnp.where(same & (lanes < rows), 1.0, 0.0), axis=1, keepdims=True)
    place_row = jnp.sum(jnp.where(same & (rows < lanes), 1.0, 0.0), axis=0, keepdims=True)

    def owner(ids):
        result = jnp.zeros_like(ids)
        for k in range(stores):
            result = jnp.where(ids == float(k), table_ref[k].astype(jnp.float32), result)
        return result

    out = []
    for ids, place in ((adapter, place_col), (as_row, place_row)):
        block = jnp.floor(place * (1.0 / SUBLANES))
        out.append((owner(ids) * SUBLANES + place - block * SUBLANES, block))
    return out


def dispatch_kernel(full, fold, per_width, stores, adapter_ref, table_ref, a_ref, b_ref, x_ref, ids_ref, row_scr):
    step = pl.program_id(0)
    tokens = adapter_ref.shape[1]
    rows = x_ref.shape[0]

    @pl.when(step == 0)
    def _():
        cols, lanes = place_tokens(adapter_ref[...].astype(jnp.float32), table_ref, stores)
        lane = lane_iota((tokens, 128))
        ids_ref[...] = jnp.where(lane == 0, cols[0], jnp.where(lane == 1, cols[1], 0.0)).astype(jnp.int32)
        row_scr[0:1, :] = lanes[0]
        row_scr[1:2, :] = lanes[1]

    at = row_scr[0:1, :].astype(jnp.int32)
    block = row_scr[1:2, :].astype(jnp.int32)
    target = row_iota((rows, tokens))

    if full:

        @pl.when(step < full * per_width)
        def _():
            pick = ((at == target) & (block == step // per_width)).astype(jnp.bfloat16)
            x_ref[...] = f32_dot(pick, a_ref[...]).astype(jnp.bfloat16)

    if fold:

        @pl.when(step >= full * per_width)
        def _():
            low = ((at == target) & (block == full)).astype(jnp.bfloat16)
            high = ((at + 4 == target) & (block == full)).astype(jnp.bfloat16)
            x_ref[...] = (f32_dot(low, a_ref[...]) + f32_dot(high, b_ref[...])).astype(jnp.bfloat16)


def dispatch(normed, token_adapter, table, full, fold):
    tokens, width = normed.shape
    stores = table.shape[0]
    column = width // 4
    per_width, half = width // column, width // 2 // column
    steps = full * per_width + fold * half

    def a_map(i):
        return (0, jnp.where(i < full * per_width, i % per_width, i - full * per_width))

    def b_map(i):
        return (0, jnp.where(i < full * per_width, half, i - full * per_width + half))

    return pl.pallas_call(
        functools.partial(dispatch_kernel, full, fold, per_width, stores),
        grid=(steps,),
        in_specs=[
            pl.BlockSpec((1, tokens), lambda i: (0, 0)),
            pl.BlockSpec(memory_space=pltpu.SMEM),
            pl.BlockSpec((tokens, column), a_map),
            pl.BlockSpec((tokens, column), b_map),
        ],
        out_specs=[
            pl.BlockSpec((stores * SUBLANES, column), lambda i: (0, i)),
            pl.BlockSpec((tokens, 128), lambda i: (0, 0)),
        ],
        out_shape=[
            jax.ShapeDtypeStruct((stores * SUBLANES, steps * column), jnp.bfloat16),
            jax.ShapeDtypeStruct((tokens, 128), jnp.int32),
        ],
        scratch_shapes=[pltpu.VMEM((8, tokens), jnp.float32)],
        compiler_params=params(),
        name="dispatch",
    )(token_adapter.reshape(1, tokens), table, normed, normed)


def project_kernel(full, fold, steps, *refs):
    refs = list(refs)
    low_refs = [(refs.pop(0), refs.pop(0)) for _ in range(full)]
    fold_ref = refs.pop(0) if fold else None
    down_low, down_high, up_kv, dkv_ref, shrunk_ref, acc = refs
    step = pl.program_id(0)
    rank = up_kv.shape[2]

    @pl.when(step == 0)
    def _():
        acc[...] = jnp.zeros_like(acc)

    low, high = down_low[0], down_high[0]
    for b, (x_low, x_high) in enumerate(low_refs):
        acc[b] += f32_dot(x_low[...], low) + f32_dot(x_high[...], high)
    if fold:
        acc[full] += f32_dot(fold_ref[...], low)
        acc[full + 1] += f32_dot(fold_ref[...], high)

    @pl.when(step == steps - 1)
    def _():
        kv_width = up_kv.shape[3]
        for b in range(full):
            shrunk = acc[b].astype(jnp.bfloat16)
            at = b * 2 * kv_width
            for i in range(2):
                piece = shrunk[:, (i + 1) * rank : (i + 2) * rank]
                dkv_ref[:, at + i * kv_width : at + (i + 1) * kv_width] = f32_dot(piece, up_kv[0, i]).astype(jnp.bfloat16)
            shrunk_ref[b] = shrunk[:, :rank]
        if fold:
            rows = acc.shape[1]
            upper = (row_iota((rows, 1)) % SUBLANES) >= 4
            mixed = jnp.where(upper, acc[full + 1], acc[full]).reshape(rows // SUBLANES, SUBLANES, 3 * rank)
            both = mixed + jnp.concatenate([mixed[:, 4:], mixed[:, :4]], axis=1)
            shrunk = both.reshape(rows, 3 * rank).astype(jnp.bfloat16)
            delta = [f32_dot(shrunk[:, (i + 1) * rank : (i + 2) * rank], up_kv[0, i]) for i in range(2)]
            dkv_ref[:, full * 2 * kv_width :] = jnp.where(upper, delta[1], delta[0]).astype(jnp.bfloat16)
            shrunk_ref[full] = shrunk[:, :rank]


def project(x, down, up_kv, full, fold):
    rows = x.shape[0]
    _, width, ranks = down.shape
    column = width // 8
    steps = width // 2 // column
    _, _, rank, kv_width = up_kv.shape
    in_specs = []
    for b in range(full):
        in_specs.append(pl.BlockSpec((rows, column), lambda i, b=b: (0, 2 * b * steps + i)))
        in_specs.append(pl.BlockSpec((rows, column), lambda i, b=b: (0, (2 * b + 1) * steps + i)))
    if fold:
        in_specs.append(pl.BlockSpec((rows, column), lambda i: (0, 2 * full * steps + i)))
    blocks = len(in_specs)
    in_specs += [
        pl.BlockSpec((1, column, ranks), lambda i: (0, i, 0)),
        pl.BlockSpec((1, column, ranks), lambda i: (0, steps + i, 0)),
        pl.BlockSpec(up_kv.shape, lambda i: (0, 0, 0, 0)),
    ]
    shapes = [(rows, (2 * full + fold) * kv_width), (full + fold, rows, rank)]
    return pl.pallas_call(
        functools.partial(project_kernel, full, fold, steps),
        grid=(steps,),
        in_specs=in_specs,
        out_specs=[pl.BlockSpec(s, lambda i, s=s: (0,) * len(s)) for s in shapes],
        out_shape=[jax.ShapeDtypeStruct(s, jnp.bfloat16) for s in shapes],
        scratch_shapes=[pltpu.VMEM((full + 2 * fold, rows, ranks), jnp.float32)],
        compiler_params=params(),
        name="project",
    )(*([x] * blocks), down, down, up_kv)


def expand_kernel(full, fold, shrunk_ref, up_ref, other_ref, out_ref):
    step = pl.program_id(0)
    rows = out_ref.shape[0]

    @pl.when(step < full * KEY_VALUE_HEADS)
    def _():
        if full:
            piece = shrunk_ref[jnp.minimum(step // KEY_VALUE_HEADS, full - 1)]
            out_ref[...] = f32_dot(piece, up_ref[0]).astype(jnp.bfloat16)

    if fold:

        @pl.when(step >= full * KEY_VALUE_HEADS)
        def _():
            upper = (row_iota((rows, 1)) % SUBLANES) >= 4
            piece = shrunk_ref[full]
            mixed = jnp.where(upper, f32_dot(piece, other_ref[0]), f32_dot(piece, up_ref[0]))
            out_ref[...] = mixed.astype(jnp.bfloat16)


def expand(shrunk, up_query, full, fold, spare):
    _, rows, rank = shrunk.shape
    width = up_query.shape[2]
    block = width // KEY_VALUE_HEADS
    half = KEY_VALUE_HEADS // 2
    steps = full * KEY_VALUE_HEADS + fold * half
    return pl.pallas_call(
        functools.partial(expand_kernel, full, fold),
        grid=(steps,),
        in_specs=[
            pl.BlockSpec(shrunk.shape, lambda i: (0, 0, 0)),
            pl.BlockSpec((1, rank, block), lambda i: (0, 0, i % KEY_VALUE_HEADS)),
            pl.BlockSpec((1, rank, block), lambda i: (0, 0, half + i % half)),
        ],
        out_specs=pl.BlockSpec((rows, block), lambda i: (0, i)),
        out_shape=jax.ShapeDtypeStruct((rows, steps * block + spare), jnp.bfloat16),
        compiler_params=params(),
        cost_estimate=cost(2 * rows * rank * steps * block * 4, 4 * rows * steps * block),
        name="expand",
    )(shrunk, up_query, up_query)


def append_kernel(rows_ref, *refs):
    refs[-1][...] = rows_ref[...]


def append(rows, into, *others):
    height, width = rows.shape
    anywhere = pl.BlockSpec(memory_space=pl.ANY)
    return pl.pallas_call(
        append_kernel,
        grid=(1,),
        in_specs=[pl.BlockSpec((height, width), lambda i: (0, 0))] + [anywhere] * (1 + len(others)),
        out_specs=pl.BlockSpec((height, width), lambda i: (0, into.shape[1] // width - 1)),
        out_shape=jax.ShapeDtypeStruct(into.shape, into.dtype),
        input_output_aliases={1: 0},
        compiler_params=params(),
        name="append",
    )(rows, into, *others)


def picks(ids, rows, block, shift):
    at, blocks = ids[:, 0:1], ids[:, 1:2]
    return ((at + shift == lane_iota((ids.shape[0], rows))) & (blocks == block)).astype(jnp.bfloat16)


def correct_kernel(full, fold, ids_ref, dkv_ref, sk_ref, sv_ref, kv_ref):
    rows = dkv_ref.shape[0]
    width = sk_ref.shape[1]
    ids = ids_ref[...]
    total = [None, None]
    for i in range(2):
        for b in range(full):
            at = (2 * b + i) * width
            term = f32_dot(picks(ids, rows, b, 0), dkv_ref[:, at : at + width])
            total[i] = term if total[i] is None else total[i] + term
        if fold:
            term = f32_dot(picks(ids, rows, full, 4 * i), dkv_ref[:, 2 * full * width :])
            total[i] = term if total[i] is None else total[i] + term
    keys = (sk_ref[...].astype(jnp.float32) + total[0]).astype(jnp.bfloat16)
    values = (sv_ref[...].astype(jnp.float32) + total[1]).astype(jnp.bfloat16)
    kv_ref[:, :width] = keys
    kv_ref[:, width:] = values


def correct(ids, dkv, shared_keys, shared_values, full, fold):
    rows, width = shared_keys.shape
    return pl.pallas_call(
        functools.partial(correct_kernel, full, fold),
        out_shape=jax.ShapeDtypeStruct((rows, 2 * width), jnp.bfloat16),
        compiler_params=params(),
        name="correct",
    )(ids, dkv, shared_keys, shared_values)


def window_chunks(kv, devices, reach):
    planes = reach // PLANE
    chunks = [(0, 0, kv)]
    for back in range(1, planes + 1):
        hop = back * PLANE
        chunks.append((back, 0, lax.ppermute(kv, "seq", [(i, i + hop) for i in range(devices - hop)])))
    bit = PLANE // 2
    while bit:
        swap = [(i, i ^ bit) for i in range(devices)]
        chunks = chunks + [(back, mark ^ bit, lax.ppermute(rows, "seq", swap)) for back, mark, rows in chunks]
        bit //= 2
    return chunks


def attend_kernel(full, fold, reach, tags, *refs):
    refs = list(refs)
    me_ref, ids_ref, request_ref, sq_ref = (refs.pop(0) for _ in range(4))
    dq_refs = [refs.pop(0) for _ in range(full + fold)]
    chunk_refs = [(refs.pop(0), refs.pop(0)) for _ in tags]
    out_ref, bias, keys, values, query, scores = refs
    head = pl.program_id(0)
    me = me_ref[0]
    tokens = sq_ref.shape[0]

    @pl.when(head == 0)
    def _():
        rows, lanes = row_iota((tokens, tokens)), lane_iota((tokens, tokens))
        own = request_ref[pl.ds(me, 1), :].astype(jnp.float32)
        own = jnp.sum(jnp.where(rows == lanes, own, 0.0), axis=1, keepdims=True)
        for at in range(reach + 1):
            source = me - reach + at
            theirs = request_ref[pl.ds(jnp.maximum(source, 0), 1), :].astype(jnp.float32)
            theirs = jnp.where(source >= 0, theirs, -1.0)
            allowed = own == theirs
            if at == reach:
                allowed = allowed & (lanes <= rows)
            bias[:, at * tokens : (at + 1) * tokens] = jnp.where(allowed, 0.0, -1e30)
        values[:, HEAD_SIZE:] = jnp.ones((values.shape[0], HEAD_SIZE), jnp.bfloat16)

    zeros = jnp.zeros((tokens, HEAD_SIZE), jnp.bfloat16)
    for at in range(reach):

        @pl.when(me - reach + at < 0)
        def _(at=at):
            keys[at * tokens : (at + 1) * tokens, :] = zeros
            values[at * tokens : (at + 1) * tokens, :HEAD_SIZE] = zeros

    for (back, mark), (k_ref, v_ref) in zip(tags, chunk_refs):
        source = (me // PLANE - back) * PLANE + jnp.bitwise_xor(me % PLANE, mark)
        at = source - me + reach

        @pl.when((source >= 0) & (at >= 0) & (at <= reach))
        def _(at=at, k_ref=k_ref, v_ref=v_ref):
            place = pl.ds(pl.multiple_of(at * tokens, tokens), tokens)
            keys[place, :] = k_ref[...]
            values[place, :HEAD_SIZE] = v_ref[...]

    ids = ids_ref[...]
    slots = dq_refs[0].shape[0]
    delta = sq_ref[...].astype(jnp.float32)
    correction = None
    for b in range(full):
        term = f32_dot(picks(ids, slots, b, 0), dq_refs[b][...])
        correction = term if correction is None else correction + term
    if fold:
        shift = 4 * (head // (KEY_VALUE_HEADS // 2))
        term = f32_dot(picks(ids, slots, full, shift), dq_refs[full][...])
        correction = term if correction is None else correction + term
    query[...] = (delta + correction).astype(jnp.bfloat16)

    factor = math.log2(math.e) / math.sqrt(HEAD_SIZE)
    heads = sq_ref.shape[1] // HEAD_SIZE

    def score(j):
        scores[j % 2] = lax.dot_general(
            query[:, j * HEAD_SIZE : (j + 1) * HEAD_SIZE],
            keys[...],
            (((1,), (1,)), ((), ())),
            preferred_element_type=jnp.float32,
        )

    score(0)
    for j in range(heads):
        if j + 1 < heads:
            score(j + 1)
        masked = scores[j % 2] + bias[...]
        raised = jnp.exp2((masked - jnp.max(masked, axis=1, keepdims=True)) * factor)
        blended = f32_dot(raised.astype(jnp.bfloat16), values[...])
        out_ref[:, j * HEAD_SIZE : (j + 1) * HEAD_SIZE] = (
            blended[:, :HEAD_SIZE] / blended[:, HEAD_SIZE:]
        ).astype(jnp.bfloat16)


def attend(me, ids, requests, shared_query, dq, chunks, full, fold, reach):
    tokens, query_width = shared_query.shape
    slots = dq.shape[0]
    block = query_width // KEY_VALUE_HEADS
    in_specs = [
        pl.BlockSpec(memory_space=pltpu.SMEM),
        pl.BlockSpec(ids.shape, lambda g: (0, 0)),
        pl.BlockSpec(requests.shape, lambda g: (0, 0)),
        pl.BlockSpec((tokens, block), lambda g: (0, g)),
    ]
    for b in range(full):
        in_specs.append(pl.BlockSpec((slots, block), lambda g, b=b: (0, b * KEY_VALUE_HEADS + g)))
    if fold:
        in_specs.append(
            pl.BlockSpec((slots, block), lambda g: (0, full * KEY_VALUE_HEADS + g % (KEY_VALUE_HEADS // 2)))
        )
    operands = [me, ids, requests, shared_query] + [dq] * (full + fold)
    for _, _, rows in chunks:
        in_specs.append(pl.BlockSpec((tokens, HEAD_SIZE), lambda g: (0, g)))
        in_specs.append(pl.BlockSpec((tokens, HEAD_SIZE), lambda g: (0, KEY_VALUE_HEADS + g)))
        operands += [rows, rows]
    window = (reach + 1) * tokens
    return pl.pallas_call(
        functools.partial(attend_kernel, full, fold, reach, tuple((b, m) for b, m, _ in chunks)),
        grid=(KEY_VALUE_HEADS,),
        in_specs=in_specs,
        out_specs=pl.BlockSpec((tokens, block), lambda g: (0, g)),
        out_shape=jax.ShapeDtypeStruct((tokens, query_width), jnp.bfloat16),
        scratch_shapes=[
            pltpu.VMEM((tokens, window), jnp.float32),
            pltpu.VMEM((window, HEAD_SIZE), jnp.bfloat16),
            pltpu.VMEM((window, 2 * HEAD_SIZE), jnp.bfloat16),
            pltpu.VMEM((tokens, block), jnp.bfloat16),
            pltpu.VMEM((2, tokens, window), jnp.float32),
        ],
        compiler_params=params(60),
        cost_estimate=cost(16 * tokens * query_width * window, 8 * tokens * query_width),
        name="attend",
    )(*operands)


def exchange(rows, devices):
    width = rows.shape[1]
    out = lax.all_to_all(
        rows.reshape(devices, rows.shape[0] // devices, width), "seq", split_axis=0, concat_axis=0, tiled=True
    )
    return out.reshape(rows.shape)


def local(
    normed,
    shared_query_rows,
    shared_key_rows,
    shared_value_rows,
    token_adapter,
    adapter_slot_table,
    adapter_down_factors,
    adapter_up_query,
    adapter_up_key_value,
    token_request,
):
    tokens = normed.shape[0]
    devices = lax.axis_size("seq")
    reach = devices // 2
    most = max(2, 3 * tokens // (2 * devices))
    fours = -(-most // 4)
    full, fold = fours // 2, fours % 2

    outgoing, ids = dispatch(normed, token_adapter, adapter_slot_table, full, fold)
    incoming = exchange(outgoing, devices)
    dkv, shrunk = project(incoming, adapter_down_factors, adapter_up_key_value, full, fold)
    dkv = exchange(dkv, devices)
    kv_width = shared_key_rows.shape[1]
    dq = expand(shrunk, adapter_up_query, full, fold, 2 * kv_width)
    kv = correct(ids, dkv, shared_key_rows, shared_value_rows, full, fold)
    chunks = window_chunks(kv, devices, reach)
    if tokens == devices * SUBLANES:
        dq = exchange(append(kv, dq, *(rows for back, mark, rows in chunks if back and not mark)), devices)
        pages = dq[:, -2 * kv_width :]
    else:
        dq = exchange(dq, devices)
        pages = exchange(kv, devices)
    me = lax.axis_index("seq").astype(jnp.int32).reshape(1)
    attention = attend(
        me, ids, token_request.reshape(devices, tokens), shared_query_rows, dq, chunks, full, fold, reach
    )
    return (attention, pages[:, :kv_width], pages[:, kv_width:])


def solution(mesh):
    rows = P(("groups", "seq"), None)
    return jax.shard_map(
        local,
        mesh=mesh,
        in_specs=(
            rows,
            rows,
            rows,
            rows,
            rows,
            P(),
            P("seq", None, None),
            P("seq", None, None),
            P("seq", None, None, None),
            P("groups"),
        ),
        out_specs=(rows, rows, rows),
        check_vma=False,
    )
```

```python
import functools
import math

import jax
import jax.numpy as jnp
from jax import lax
from jax.experimental import pallas as pl
from jax.experimental.pallas import tpu as pltpu
from jax.sharding import PartitionSpec as P

KEY_VALUE_HEADS = 4
HEAD_SIZE = 128
SUBLANES = 8
PLANE = 4
MIB = 1024 * 1024


def params(mib=40):
    return pltpu.CompilerParams(vmem_limit_bytes=mib * MIB)


def cost(flops, moved):
    return pl.CostEstimate(flops=flops, bytes_accessed=moved, transcendentals=0)


def f32_dot(a, b):
    return jnp.dot(a, b, preferred_element_type=jnp.float32)


def lane_iota(shape):
    return lax.broadcasted_iota(jnp.int32, shape, 1)


def turned_dot(a, b):
    return lax.dot_general(a, b, (((1,), (1,)), ((), ())), preferred_element_type=jnp.float32)


def row_iota(shape):
    return lax.broadcasted_iota(jnp.int32, shape, 0)


def place_tokens(as_row, table_ref, stores):
    count = as_row.shape[1]
    rows, lanes = row_iota((count, count)), lane_iota((count, count))
    adapter = jnp.sum(jnp.where(rows == lanes, as_row, 0.0), axis=1, keepdims=True)
    same = adapter == as_row
    place_col = jnp.sum(jnp.where(same & (lanes < rows), 1.0, 0.0), axis=1, keepdims=True)
    place_row = jnp.sum(jnp.where(same & (rows < lanes), 1.0, 0.0), axis=0, keepdims=True)

    def owner(ids):
        result = jnp.zeros_like(ids)
        for k in range(stores):
            result = jnp.where(ids == float(k), table_ref[k].astype(jnp.float32), result)
        return result

    out = []
    for ids, place in ((adapter, place_col), (as_row, place_row)):
        block = jnp.floor(place * (1.0 / SUBLANES))
        out.append((owner(ids) * SUBLANES + place - block * SUBLANES, block))
    return out


def dispatch_kernel(full, fold, per_width, stores, adapter_ref, table_ref, a_ref, b_ref, x_ref, ids_ref, row_scr):
    step = pl.program_id(0)
    tokens = adapter_ref.shape[1]
    rows = x_ref.shape[0]

    @pl.when(step == 0)
    def _():
        cols, lanes = place_tokens(adapter_ref[...].astype(jnp.float32), table_ref, stores)
        lane = lane_iota((tokens, 128))
        ids_ref[...] = jnp.where(lane == 0, cols[0], jnp.where(lane == 1, cols[1], 0.0)).astype(jnp.int32)
        row_scr[0:1, :] = lanes[0]
        row_scr[1:2, :] = lanes[1]

    at = row_scr[0:1, :].astype(jnp.int32)
    block = row_scr[1:2, :].astype(jnp.int32)
    target = row_iota((rows, tokens))

    if full:

        @pl.when(step < full * per_width)
        def _():
            pick = ((at == target) & (block == step // per_width)).astype(jnp.bfloat16)
            x_ref[...] = f32_dot(pick, a_ref[...]).astype(jnp.bfloat16)

    if fold:

        @pl.when(step >= full * per_width)
        def _():
            low = ((at == target) & (block == full)).astype(jnp.bfloat16)
            high = ((at + 4 == target) & (block == full)).astype(jnp.bfloat16)
            x_ref[...] = (f32_dot(low, a_ref[...]) + f32_dot(high, b_ref[...])).astype(jnp.bfloat16)


def dispatch(normed, token_adapter, table, full, fold):
    tokens, width = normed.shape
    stores = table.shape[0]
    column = width // 4
    per_width, half = width // column, width // 2 // column
    steps = full * per_width + fold * half

    def a_map(i):
        return (0, jnp.where(i < full * per_width, i % per_width, i - full * per_width))

    def b_map(i):
        return (0, jnp.where(i < full * per_width, half, i - full * per_width + half))

    return pl.pallas_call(
        functools.partial(dispatch_kernel, full, fold, per_width, stores),
        grid=(steps,),
        in_specs=[
            pl.BlockSpec((1, tokens), lambda i: (0, 0)),
            pl.BlockSpec(memory_space=pltpu.SMEM),
            pl.BlockSpec((tokens, column), a_map),
            pl.BlockSpec((tokens, column), b_map),
        ],
        out_specs=[
            pl.BlockSpec((stores * SUBLANES, column), lambda i: (0, i)),
            pl.BlockSpec((tokens, 128), lambda i: (0, 0)),
        ],
        out_shape=[
            jax.ShapeDtypeStruct((stores * SUBLANES, steps * column), jnp.bfloat16),
            jax.ShapeDtypeStruct((tokens, 128), jnp.int32),
        ],
        scratch_shapes=[pltpu.VMEM((8, tokens), jnp.float32)],
        compiler_params=params(),
        name="dispatch",
    )(token_adapter.reshape(1, tokens), table, normed, normed)


def project_kernel(full, fold, steps, *refs):
    refs = list(refs)
    low_refs = [(refs.pop(0), refs.pop(0)) for _ in range(full)]
    fold_ref = refs.pop(0) if fold else None
    (down_low, down_high, up_kv), (out_ref, acc) = refs[:3], refs[-2:]
    step = pl.program_id(0)
    rank = up_kv.shape[2]

    @pl.when(step == 0)
    def _():
        acc[...] = jnp.zeros_like(acc)

    low, high = down_low[0], down_high[0]
    for b, (x_low, x_high) in enumerate(low_refs):
        acc[b] += turned_dot(x_low[...], low) + turned_dot(x_high[...], high)
    if fold:
        acc[full] += turned_dot(fold_ref[...], low)
        acc[full + 1] += turned_dot(fold_ref[...], high)

    @pl.when(step == steps - 1)
    def _():
        kv_width = up_kv.shape[3]
        queries = []
        for b in range(full):
            shrunk = acc[b].astype(jnp.bfloat16)
            at = b * 2 * kv_width
            for i in range(2):
                piece = shrunk[:, (i + 1) * rank : (i + 2) * rank]
                out_ref[:, at + i * kv_width : at + (i + 1) * kv_width] = f32_dot(piece, up_kv[0, i]).astype(jnp.bfloat16)
            queries.append(shrunk[:, :rank])
        if fold:
            rows = acc.shape[1]
            upper = (row_iota((rows, 1)) % SUBLANES) >= 4
            mixed = jnp.where(upper, acc[full + 1], acc[full]).reshape(rows // SUBLANES, SUBLANES, 3 * rank)
            both = mixed + jnp.concatenate([mixed[:, 4:], mixed[:, :4]], axis=1)
            shrunk = both.reshape(rows, 3 * rank).astype(jnp.bfloat16)
            delta = [f32_dot(shrunk[:, (i + 1) * rank : (i + 2) * rank], up_kv[0, i]) for i in range(2)]
            at = full * 2 * kv_width
            out_ref[:, at : at + kv_width] = jnp.where(upper, delta[1], delta[0]).astype(jnp.bfloat16)
            queries.append(shrunk[:, :rank])
        if len(queries) % 2:
            queries.append(jnp.zeros_like(queries[0]))
        out_ref[:, (2 * full + fold) * kv_width :] = jnp.concatenate(queries, axis=1)


def project(x, down, up_kv, full, fold, *others):
    rows = x.shape[0]
    _, ranks, width = down.shape
    column = width // 8
    steps = width // 2 // column
    _, _, rank, kv_width = up_kv.shape
    in_specs = []
    for b in range(full):
        in_specs.append(pl.BlockSpec((rows, column), lambda i, b=b: (0, 2 * b * steps + i)))
        in_specs.append(pl.BlockSpec((rows, column), lambda i, b=b: (0, (2 * b + 1) * steps + i)))
    if fold:
        in_specs.append(pl.BlockSpec((rows, column), lambda i: (0, 2 * full * steps + i)))
    blocks = len(in_specs)
    in_specs += [
        pl.BlockSpec((1, ranks, column), lambda i: (0, 0, i)),
        pl.BlockSpec((1, ranks, column), lambda i: (0, 0, steps + i)),
        pl.BlockSpec(up_kv.shape, lambda i: (0, 0, 0, 0)),
    ]
    in_specs += [pl.BlockSpec(memory_space=pltpu.HBM)] * len(others)
    shape = (rows, (2 * full + fold) * kv_width + (full + fold + 1) // 2 * 2 * rank)
    return pl.pallas_call(
        functools.partial(project_kernel, full, fold, steps),
        grid=(steps,),
        in_specs=in_specs,
        out_specs=pl.BlockSpec(shape, lambda i: (0, 0)),
        out_shape=jax.ShapeDtypeStruct(shape, jnp.bfloat16),
        scratch_shapes=[pltpu.VMEM((full + 2 * fold, rows, ranks), jnp.float32)],
        compiler_params=params(),
        name="project",
    )(*([x] * blocks), down, down, up_kv, *others)


def picks(at, chosen, rows):
    return ((at == lane_iota((at.shape[0], rows))) & chosen).astype(jnp.bfloat16)


def correct_kernel(full, fold, rank, ids_ref, back_ref, sk_ref, sv_ref, kv_ref, shrunk_ref):
    rows = back_ref.shape[0]
    width = sk_ref.shape[1]
    place, block = ids_ref[:, 0:1], ids_ref[:, 1:2]
    queries = (2 * full + fold) * width
    total = [0.0, 0.0, 0.0]
    for b in range(full + fold):
        pick = picks(place, block == b, rows)
        for i in range(2):
            if b < full:
                at = (2 * b + i) * width
            else:
                at = 2 * full * width
                pick = pick if i == 0 else picks(place + 4, block == b, rows)
            total[i] += f32_dot(pick, back_ref[:, at : at + width])
    for b in range(full + fold):
        at = queries + b // 2 * 2 * rank
        both = f32_dot(picks(place, block == b, rows), back_ref[:, at : at + 2 * rank])
        total[2] += both if b % 2 == 0 else pltpu.roll(both, rank, 1)
    kv_ref[:, :width] = (sk_ref[...].astype(jnp.float32) + total[0]).astype(jnp.bfloat16)
    kv_ref[:, width:] = (sv_ref[...].astype(jnp.float32) + total[1]).astype(jnp.bfloat16)
    lanes = lane_iota(shrunk_ref.shape)
    owner = (place // SUBLANES).astype(jnp.float32)
    shrunk_ref[...] = jnp.where(lanes < rank, total[2], jnp.where(lanes == rank, owner, 0.0)).astype(jnp.bfloat16)


def correct(ids, back, shared_keys, shared_values, rank, full, fold):
    rows, width = shared_keys.shape
    return pl.pallas_call(
        functools.partial(correct_kernel, full, fold, rank),
        out_shape=[
            jax.ShapeDtypeStruct((rows, 2 * width), jnp.bfloat16),
            jax.ShapeDtypeStruct((rows, 2 * rank), jnp.bfloat16),
        ],
        compiler_params=params(),
        name="correct",
    )(ids, back, shared_keys, shared_values)


def expand_kernel(marks, me_ref, *refs):
    shrunk_refs, refs = refs[:2], refs[2:]
    up_refs, refs = refs[: len(marks)], refs[len(marks) :]
    own_ref, far_refs, (wide, ups) = refs[0], refs[1:-2], refs[-2:]
    rank = up_refs[0].shape[0]
    tokens = own_ref.shape[0]

    @pl.when(pl.program_id(0) == 0)
    def _():
        lanes = lane_iota((tokens, 2 * rank))
        for i, shrunk_ref in enumerate(shrunk_refs):
            rows = shrunk_ref[...].astype(jnp.float32)
            apart = jnp.bitwise_xor(rows[:, rank : rank + 1].astype(jnp.int32), me_ref[0])
            twice = jnp.where(lanes < rank, rows, pltpu.roll(rows, rank, 1))
            for k in range(0, len(marks), 2):
                wanted = jnp.where(lanes < rank, marks[k], marks[k + 1])
                held = jnp.where(apart == wanted, twice, 0.0).astype(jnp.bfloat16)
                wide[i * tokens : (i + 1) * tokens, k * rank : (k + 2) * rank] = held

    for k, up_ref in enumerate(up_refs):
        ups[k * rank : (k + 1) * rank, :] = up_ref[...]
    result = f32_dot(wide[...], ups[...]).astype(jnp.bfloat16)
    own_ref[...] = result[:tokens]
    for i, far_ref in enumerate(far_refs):

        @pl.when(pl.program_id(0) == i)
        def _(far_ref=far_ref):
            far_ref[...] = result[tokens:]


def expand(me, shrunk, far_shrunk, ups):
    tokens = shrunk.shape[0]
    marks = tuple(sorted(ups))
    rank, width = ups[0].shape
    block = width // KEY_VALUE_HEADS
    whole = pl.BlockSpec(shrunk.shape, lambda g: (0, 0))
    part = pl.BlockSpec((tokens, block), lambda g: (0, g))
    return pl.pallas_call(
        functools.partial(expand_kernel, marks),
        grid=(KEY_VALUE_HEADS,),
        in_specs=[pl.BlockSpec(memory_space=pltpu.SMEM), whole, whole]
        + [pl.BlockSpec((rank, block), lambda g: (0, g))] * len(marks),
        out_specs=[part] + [pl.BlockSpec((tokens, block), lambda g: (0, 0))] * KEY_VALUE_HEADS,
        out_shape=[jax.ShapeDtypeStruct((tokens, width), jnp.bfloat16)]
        + [jax.ShapeDtypeStruct((tokens, block), jnp.bfloat16)] * KEY_VALUE_HEADS,
        scratch_shapes=[
            pltpu.VMEM((2 * tokens, len(marks) * rank), jnp.bfloat16),
            pltpu.VMEM((len(marks) * rank, block), jnp.bfloat16),
        ],
        compiler_params=params(60),
        cost_estimate=cost(16 * tokens * len(marks) * rank * width, 4 * tokens * width),
        name="expand",
    )(me, shrunk, far_shrunk, *(ups[k] for k in marks))


def token_kernel(*refs):
    refs[-1][...] = jnp.zeros_like(refs[-1])


def token(*others):
    return pl.pallas_call(
        token_kernel,
        in_specs=[pl.BlockSpec(memory_space=pltpu.HBM)] * len(others),
        out_specs=pl.BlockSpec(memory_space=pltpu.VMEM),
        out_shape=jax.ShapeDtypeStruct((SUBLANES, 128), jnp.float32),
        compiler_params=params(62),
        name="token",
    )(*others)


def hold(rows, *others):
    anywhere = pl.BlockSpec(memory_space=pl.ANY)
    return pl.pallas_call(
        lambda *refs: None,
        in_specs=[anywhere] + [pl.BlockSpec(memory_space=pltpu.HBM)] * len(others),
        out_specs=anywhere,
        out_shape=jax.ShapeDtypeStruct(rows.shape, rows.dtype),
        input_output_aliases={0: 0},
        compiler_params=params(),
        name="hold",
    )(rows, *others)


def swap_pairs(devices, distance):
    return [(i, i ^ distance) for i in range(devices)]


def mirrored(rows, devices):
    return lax.ppermute(rows, "seq", swap_pairs(devices, devices // 2))


def crossed(factors, devices):
    if lax.axis_size("groups") != 2:
        return mirrored(factors, devices)
    half = factors.shape[1] // 2
    return mirrored(jnp.where(lax.axis_index("groups") == 0, factors[:, :half], factors[:, half:]), devices)


def gathered_factors(factors, here, devices):
    if here.shape != factors.shape:
        first = lax.axis_index("groups") == 0
        there = lax.ppermute(here, "groups", [(0, 1), (1, 0)])
        here = jnp.concatenate([jnp.where(first, here, there), jnp.where(first, there, here)], axis=1)
    held = {0: factors, devices // 2: here}
    bit = devices // 4
    while bit:
        if bit != PLANE:
            swap = swap_pairs(devices, bit)
            held.update({k ^ bit: lax.ppermute(a, "seq", swap) for k, a in list(held.items())})
        bit //= 2
    return held


def window_chunks(kv, devices, reach):
    chunks = [(0, 0, kv)]
    for back in range(1, reach // PLANE + 1):
        hop = back * PLANE
        chunks.append((back, 0, lax.ppermute(kv, "seq", [(i, i + hop) for i in range(devices - hop)])))
    bit = PLANE // 2
    while bit:
        swap = swap_pairs(devices, bit)
        chunks = chunks + [(back, mark ^ bit, lax.ppermute(rows, "seq", swap)) for back, mark, rows in chunks]
        bit //= 2
    return chunks


def attend_kernel(reach, tags, *refs):
    me_ref, request_ref, sq_ref, own_ref = refs[:4]
    far_refs, refs = refs[4 : 4 + KEY_VALUE_HEADS], refs[4 + KEY_VALUE_HEADS :]
    chunk_refs = [(refs[2 * i], refs[2 * i + 1]) for i in range(len(tags))]
    out_ref, bias, keys, values, query, scores = refs[2 * len(tags) :]
    head = pl.program_id(0)
    me = me_ref[0]
    tokens = sq_ref.shape[0]
    for i, far_ref in enumerate(far_refs):

        @pl.when(head == i)
        def _(far_ref=far_ref):
            correction = own_ref[...].astype(jnp.float32) + far_ref[...].astype(jnp.float32)
            query[...] = (sq_ref[...].astype(jnp.float32) + correction).astype(jnp.bfloat16)

    @pl.when(head == 0)
    def _():
        rows, lanes = row_iota((tokens, tokens)), lane_iota((tokens, tokens))
        own = request_ref[pl.ds(me, 1), :].astype(jnp.float32)
        own = jnp.sum(jnp.where(rows == lanes, own, 0.0), axis=1, keepdims=True)
        for at in range(reach + 1):
            source = me - reach + at
            theirs = request_ref[pl.ds(jnp.maximum(source, 0), 1), :].astype(jnp.float32)
            theirs = jnp.where(source >= 0, theirs, -1.0)
            allowed = own == theirs
            if at == reach:
                allowed = allowed & (lanes <= rows)
            bias[:, at * tokens : (at + 1) * tokens] = jnp.where(allowed, 0.0, -1e30)
        values[:, HEAD_SIZE:] = jnp.ones((values.shape[0], HEAD_SIZE), jnp.bfloat16)

    zeros = jnp.zeros((tokens, HEAD_SIZE), jnp.bfloat16)
    for at in range(reach):

        @pl.when(me - reach + at < 0)
        def _(at=at):
            keys[at * tokens : (at + 1) * tokens, :] = zeros
            values[at * tokens : (at + 1) * tokens, :HEAD_SIZE] = zeros

    for (back, mark), (k_ref, v_ref) in zip(tags, chunk_refs):
        source = (me // PLANE - back) * PLANE + jnp.bitwise_xor(me % PLANE, mark)
        at = source - me + reach

        @pl.when((source >= 0) & (at >= 0) & (at <= reach))
        def _(at=at, k_ref=k_ref, v_ref=v_ref):
            place = pl.ds(pl.multiple_of(at * tokens, tokens), tokens)
            keys[place, :] = k_ref[...]
            values[place, :HEAD_SIZE] = v_ref[...]

    factor = math.log2(math.e) / math.sqrt(HEAD_SIZE)
    heads = query.shape[1] // HEAD_SIZE

    def score(j):
        scores[j % 2] = lax.dot_general(
            query[:, j * HEAD_SIZE : (j + 1) * HEAD_SIZE],
            keys[...],
            (((1,), (1,)), ((), ())),
            preferred_element_type=jnp.float32,
        )

    score(0)
    for j in range(heads):
        if j + 1 < heads:
            score(j + 1)
        masked = scores[j % 2] + bias[...]
        raised = jnp.exp2((masked - jnp.max(masked, axis=1, keepdims=True)) * factor)
        blended = f32_dot(raised.astype(jnp.bfloat16), values[...])
        out_ref[:, j * HEAD_SIZE : (j + 1) * HEAD_SIZE] = (
            blended[:, :HEAD_SIZE] / blended[:, HEAD_SIZE:]
        ).astype(jnp.bfloat16)


def attend(me, requests, shared_query, own, far, chunks, reach):
    tokens, query_width = shared_query.shape
    block = query_width // KEY_VALUE_HEADS
    in_specs = [
        pl.BlockSpec(memory_space=pltpu.SMEM),
        pl.BlockSpec(requests.shape, lambda g: (0, 0)),
        pl.BlockSpec((tokens, block), lambda g: (0, g)),
        pl.BlockSpec((tokens, block), lambda g: (0, g)),
    ] + [pl.BlockSpec((tokens, block), lambda g: (0, 0))] * len(far)
    operands = [me, requests, shared_query, own, *far]
    for _, _, rows in chunks:
        in_specs.append(pl.BlockSpec((tokens, HEAD_SIZE), lambda g: (0, g)))
        in_specs.append(pl.BlockSpec((tokens, HEAD_SIZE), lambda g: (0, KEY_VALUE_HEADS + g)))
        operands += [rows, rows]
    window = (reach + 1) * tokens
    return pl.pallas_call(
        functools.partial(attend_kernel, reach, tuple((b, m) for b, m, _ in chunks)),
        grid=(KEY_VALUE_HEADS,),
        in_specs=in_specs,
        out_specs=pl.BlockSpec((tokens, block), lambda g: (0, g)),
        out_shape=jax.ShapeDtypeStruct((tokens, query_width), jnp.bfloat16),
        scratch_shapes=[
            pltpu.VMEM((tokens, window), jnp.float32),
            pltpu.VMEM((window, HEAD_SIZE), jnp.bfloat16),
            pltpu.VMEM((window, 2 * HEAD_SIZE), jnp.bfloat16),
            pltpu.VMEM((tokens, block), jnp.bfloat16),
            pltpu.VMEM((2, tokens, window), jnp.float32),
        ],
        compiler_params=params(60),
        cost_estimate=cost(16 * tokens * query_width * window, 8 * tokens * query_width),
        name="attend",
    )(*operands)


def exchange(rows, devices):
    width = rows.shape[1]
    out = lax.all_to_all(
        rows.reshape(devices, rows.shape[0] // devices, width), "seq", split_axis=0, concat_axis=0, tiled=True
    )
    return out.reshape(rows.shape)


def local(
    normed,
    shared_query_rows,
    shared_key_rows,
    shared_value_rows,
    token_adapter,
    adapter_slot_table,
    adapter_down_factors,
    adapter_up_query,
    adapter_up_key_value,
    token_request,
):
    tokens = normed.shape[0]
    devices = lax.axis_size("seq")
    reach = devices // 2
    most = max(2, 3 * tokens // (2 * devices))
    fours = -(-most // 4)
    full, fold = fours // 2, fours % 2

    me = lax.axis_index("seq").astype(jnp.int32).reshape(1)
    factors = adapter_up_query[0]
    rank = factors.shape[0]
    here = crossed(factors, devices)
    outgoing, ids = dispatch(normed, token_adapter, adapter_slot_table, full, fold)
    incoming = exchange(hold(outgoing, here), devices)
    ups = gathered_factors(factors, here, devices)
    early = [token(*(ups[k] for k in ups if k))]
    back = exchange(project(incoming, jnp.swapaxes(adapter_down_factors, 1, 2), adapter_up_key_value, full, fold, *early), devices)
    kv, shrunk = correct(ids, back, shared_key_rows, shared_value_rows, rank, full, fold)
    swap = swap_pairs(devices, PLANE)
    own, *far = expand(me, shrunk, lax.ppermute(shrunk, "seq", swap), ups)
    chunks = window_chunks(kv, devices, reach)
    pages = exchange(kv, devices)
    far = [lax.ppermute(a, "seq", swap) for a in far]
    requests = token_request.reshape(devices, tokens)
    attention = attend(me, requests, shared_query_rows, own, far, chunks, reach)
    width = pages.shape[1] // 2
    return (attention, pages[:, :width], pages[:, width:])


def solution(mesh):
    rows = P(("groups", "seq"), None)
    return jax.shard_map(
        local,
        mesh=mesh,
        in_specs=(
            rows,
            rows,
            rows,
            rows,
            rows,
            P(),
            P("seq", None, None),
            P("seq", None, None),
            P("seq", None, None, None),
            P("groups"),
        ),
        out_specs=(rows, rows, rows),
        check_vma=False,
    )
```

```python
import functools
import math

import jax
import jax.numpy as jnp
from jax import lax
from jax.experimental import pallas as pl
from jax.experimental.pallas import tpu as pltpu
from jax.sharding import PartitionSpec as P

KEY_VALUE_HEADS = 4
HEAD_SIZE = 128
SUBLANES = 8
PLANE = 4
FAR_PARTS = 1
ATTEND_CALLS = 1
MIB = 1024 * 1024


def params(mib=40):
    return pltpu.CompilerParams(vmem_limit_bytes=mib * MIB)


def cost(flops, moved):
    return pl.CostEstimate(flops=flops, bytes_accessed=moved, transcendentals=0)


def f32_dot(a, b):
    return jnp.dot(a, b, preferred_element_type=jnp.float32)


def lane_iota(shape):
    return lax.broadcasted_iota(jnp.int32, shape, 1)


def row_iota(shape):
    return lax.broadcasted_iota(jnp.int32, shape, 0)


def place_tokens(as_row, table_ref, stores):
    count = as_row.shape[1]
    rows, lanes = row_iota((count, count)), lane_iota((count, count))
    adapter = jnp.sum(jnp.where(rows == lanes, as_row, 0.0), axis=1, keepdims=True)
    same = adapter == as_row
    place_col = jnp.sum(jnp.where(same & (lanes < rows), 1.0, 0.0), axis=1, keepdims=True)
    place_row = jnp.sum(jnp.where(same & (rows < lanes), 1.0, 0.0), axis=0, keepdims=True)

    def owner(ids):
        result = jnp.zeros_like(ids)
        for k in range(stores):
            result = jnp.where(ids == float(k), table_ref[k].astype(jnp.float32), result)
        return result

    out = []
    for ids, place in ((adapter, place_col), (as_row, place_row)):
        block = jnp.floor(place * (1.0 / SUBLANES))
        out.append((owner(ids) * SUBLANES + place - block * SUBLANES, block))
    return out


def dispatch_kernel(full, fold, per_width, stores, adapter_ref, table_ref, a_ref, b_ref, x_ref, ids_ref, row_scr):
    step = pl.program_id(0)
    tokens = adapter_ref.shape[1]
    rows = x_ref.shape[0]

    @pl.when(step == 0)
    def _():
        cols, lanes = place_tokens(adapter_ref[...].astype(jnp.float32), table_ref, stores)
        lane = lane_iota((tokens, 128))
        ids_ref[...] = jnp.where(lane == 0, cols[0], jnp.where(lane == 1, cols[1], 0.0)).astype(jnp.int32)
        row_scr[0:1, :] = lanes[0]
        row_scr[1:2, :] = lanes[1]

    at = row_scr[0:1, :].astype(jnp.int32)
    block = row_scr[1:2, :].astype(jnp.int32)
    target = row_iota((rows, tokens))

    if full:

        @pl.when(step < full * per_width)
        def _():
            pick = ((at == target) & (block == step // per_width)).astype(jnp.bfloat16)
            x_ref[...] = f32_dot(pick, a_ref[...]).astype(jnp.bfloat16)

    if fold:

        @pl.when(step >= full * per_width)
        def _():
            low = ((at == target) & (block == full)).astype(jnp.bfloat16)
            high = ((at + 4 == target) & (block == full)).astype(jnp.bfloat16)
            x_ref[...] = (f32_dot(low, a_ref[...]) + f32_dot(high, b_ref[...])).astype(jnp.bfloat16)


def dispatch(normed, token_adapter, table, full, fold):
    tokens, width = normed.shape
    stores = table.shape[0]
    column = width // 4
    per_width, half = width // column, width // 2 // column
    steps = full * per_width + fold * half

    def a_map(i):
        return (0, jnp.where(i < full * per_width, i % per_width, i - full * per_width))

    def b_map(i):
        return (0, jnp.where(i < full * per_width, half, i - full * per_width + half))

    return pl.pallas_call(
        functools.partial(dispatch_kernel, full, fold, per_width, stores),
        grid=(steps,),
        in_specs=[
            pl.BlockSpec((1, tokens), lambda i: (0, 0)),
            pl.BlockSpec(memory_space=pltpu.SMEM),
            pl.BlockSpec((tokens, column), a_map),
            pl.BlockSpec((tokens, column), b_map),
        ],
        out_specs=[
            pl.BlockSpec((stores * SUBLANES, column), lambda i: (0, i)),
            pl.BlockSpec((tokens, 128), lambda i: (0, 0)),
        ],
        out_shape=[
            jax.ShapeDtypeStruct((stores * SUBLANES, steps * column), jnp.bfloat16),
            jax.ShapeDtypeStruct((tokens, 128), jnp.int32),
        ],
        scratch_shapes=[pltpu.VMEM((8, tokens), jnp.float32)],
        compiler_params=params(),
        name="dispatch",
    )(token_adapter.reshape(1, tokens), table, normed, normed)


def project_kernel(full, fold, steps, *refs):
    refs = list(refs)
    low_refs = [(refs.pop(0), refs.pop(0)) for _ in range(full)]
    fold_ref = refs.pop(0) if fold else None
    (down_low, down_high, up_kv), (out_ref, acc) = refs[:3], refs[-2:]
    step = pl.program_id(0)
    rank = up_kv.shape[2]

    @pl.when(step == 0)
    def _():
        acc[...] = jnp.zeros_like(acc)

    low, high = down_low[0], down_high[0]
    for b, (x_low, x_high) in enumerate(low_refs):
        acc[b] += f32_dot(x_low[...], low) + f32_dot(x_high[...], high)
    if fold:
        acc[full] += f32_dot(fold_ref[...], low)
        acc[full + 1] += f32_dot(fold_ref[...], high)

    @pl.when(step == steps - 1)
    def _():
        kv_width = up_kv.shape[3]
        queries = []
        for b in range(full):
            shrunk = acc[b].astype(jnp.bfloat16)
            at = b * 2 * kv_width
            for i in range(2):
                piece = shrunk[:, (i + 1) * rank : (i + 2) * rank]
                out_ref[:, at + i * kv_width : at + (i + 1) * kv_width] = f32_dot(piece, up_kv[0, i]).astype(jnp.bfloat16)
            queries.append(shrunk[:, :rank])
        if fold:
            rows = acc.shape[1]
            upper = (row_iota((rows, 1)) % SUBLANES) >= 4
            mixed = jnp.where(upper, acc[full + 1], acc[full]).reshape(rows // SUBLANES, SUBLANES, 3 * rank)
            both = mixed + jnp.concatenate([mixed[:, 4:], mixed[:, :4]], axis=1)
            shrunk = both.reshape(rows, 3 * rank).astype(jnp.bfloat16)
            delta = [f32_dot(shrunk[:, (i + 1) * rank : (i + 2) * rank], up_kv[0, i]) for i in range(2)]
            at = full * 2 * kv_width
            out_ref[:, at : at + kv_width] = jnp.where(upper, delta[1], delta[0]).astype(jnp.bfloat16)
            queries.append(shrunk[:, :rank])
        if len(queries) % 2:
            queries.append(jnp.zeros_like(queries[0]))
        out_ref[:, (2 * full + fold) * kv_width :] = jnp.concatenate(queries, axis=1)


def project(x, down, up_kv, full, fold, *others):
    rows = x.shape[0]
    _, width, ranks = down.shape
    column = width // 8
    steps = width // 2 // column
    _, _, rank, kv_width = up_kv.shape
    in_specs = []
    for b in range(full):
        in_specs.append(pl.BlockSpec((rows, column), lambda i, b=b: (0, 2 * b * steps + i)))
        in_specs.append(pl.BlockSpec((rows, column), lambda i, b=b: (0, (2 * b + 1) * steps + i)))
    if fold:
        in_specs.append(pl.BlockSpec((rows, column), lambda i: (0, 2 * full * steps + i)))
    blocks = len(in_specs)
    in_specs += [
        pl.BlockSpec((1, column, ranks), lambda i: (0, i, 0)),
        pl.BlockSpec((1, column, ranks), lambda i: (0, steps + i, 0)),
        pl.BlockSpec(up_kv.shape, lambda i: (0, 0, 0, 0)),
    ]
    in_specs += [pl.BlockSpec(memory_space=pltpu.HBM)] * len(others)
    shape = (rows, (2 * full + fold) * kv_width + (full + fold + 1) // 2 * 2 * rank)
    return pl.pallas_call(
        functools.partial(project_kernel, full, fold, steps),
        grid=(steps,),
        in_specs=in_specs,
        out_specs=pl.BlockSpec(shape, lambda i: (0, 0)),
        out_shape=jax.ShapeDtypeStruct(shape, jnp.bfloat16),
        scratch_shapes=[pltpu.VMEM((full + 2 * fold, rows, ranks), jnp.float32)],
        compiler_params=params(),
        name="project",
    )(*([x] * blocks), down, down, up_kv, *others)


def picks(at, chosen, rows):
    return ((at == lane_iota((at.shape[0], rows))) & chosen).astype(jnp.bfloat16)


def correct_kernel(full, fold, rank, ids_ref, back_ref, sk_ref, sv_ref, kv_ref, shrunk_ref):
    rows = back_ref.shape[0]
    width = sk_ref.shape[1]
    place, block = ids_ref[:, 0:1], ids_ref[:, 1:2]
    queries = (2 * full + fold) * width
    total = [0.0, 0.0, 0.0]
    for b in range(full + fold):
        pick = picks(place, block == b, rows)
        for i in range(2):
            if b < full:
                at = (2 * b + i) * width
            else:
                at = 2 * full * width
                pick = pick if i == 0 else picks(place + 4, block == b, rows)
            total[i] += f32_dot(pick, back_ref[:, at : at + width])
    for b in range(full + fold):
        at = queries + b // 2 * 2 * rank
        both = f32_dot(picks(place, block == b, rows), back_ref[:, at : at + 2 * rank])
        total[2] += both if b % 2 == 0 else pltpu.roll(both, rank, 1)
    kv_ref[:, :width] = (sk_ref[...].astype(jnp.float32) + total[0]).astype(jnp.bfloat16)
    kv_ref[:, width:] = (sv_ref[...].astype(jnp.float32) + total[1]).astype(jnp.bfloat16)
    lanes = lane_iota(shrunk_ref.shape)
    owner = (place // SUBLANES).astype(jnp.float32)
    shrunk_ref[...] = jnp.where(lanes < rank, total[2], jnp.where(lanes == rank, owner, 0.0)).astype(jnp.bfloat16)


def correct(ids, back, shared_keys, shared_values, rank, full, fold):
    rows, width = shared_keys.shape
    return pl.pallas_call(
        functools.partial(correct_kernel, full, fold, rank),
        out_shape=[
            jax.ShapeDtypeStruct((rows, 2 * width), jnp.bfloat16),
            jax.ShapeDtypeStruct((rows, 2 * rank), jnp.bfloat16),
        ],
        compiler_params=params(),
        name="correct",
    )(ids, back, shared_keys, shared_values)


def packing(owner, me, rows):
    tokens = owner.shape[0]
    held = jnp.bitwise_and(jnp.bitwise_xor(owner, me), PLANE) == 0
    flags = jnp.broadcast_to(held.astype(jnp.float32), (tokens, tokens)).astype(jnp.bfloat16)
    before = (lane_iota((tokens, tokens)) < row_iota((tokens, tokens))).astype(jnp.bfloat16)
    place = f32_dot(before, flags)[:, :1].astype(jnp.int32)
    return ((place == lane_iota((tokens, rows))) & held).astype(jnp.bfloat16)


def expand_kernel(marks, me_ref, own_rows_ref, far_rows_ref, kv_ref, *refs):
    up_refs, refs = refs[: len(marks)], refs[len(marks) :]
    (own_ref, unpack_ref, pages_ref), far_refs, (wide, ups) = refs[:3], refs[3:-2], refs[-2:]
    rank = up_refs[0].shape[0]
    tokens, packed = unpack_ref.shape

    @pl.when(pl.program_id(0) == 0)
    def _():
        me = me_ref[0]
        pages_ref[...] = kv_ref[...]

        def owners(rows):
            return rows[:, rank : rank + 1].astype(jnp.float32).astype(jnp.int32)

        def widen(rows, owner, at):
            count = rows.shape[0]
            lanes = lane_iota((count, 2 * rank))
            apart = jnp.bitwise_xor(owner, me)
            twice = jnp.where(lanes < rank, rows, pltpu.roll(rows, rank, 1))
            for k in range(0, len(marks), 2):
                wanted = jnp.where(lanes < rank, marks[k], marks[k + 1])
                held = jnp.where(apart == wanted, twice, 0.0).astype(jnp.bfloat16)
                wide[at : at + count, k * rank : (k + 2) * rank] = held

        own_rows, far_rows = own_rows_ref[...], far_rows_ref[...]
        own_owner = owners(own_rows)
        unpack_ref[...] = packing(own_owner, jnp.bitwise_xor(me, PLANE), packed)
        widen(own_rows.astype(jnp.float32), own_owner, 0)
        pack = packing(owners(far_rows), me, packed)
        far_rows = lax.dot_general(pack, far_rows, (((0,), (0,)), ((), ())), preferred_element_type=jnp.float32)
        widen(far_rows, owners(far_rows), tokens)

    for k, up_ref in enumerate(up_refs):
        ups[k * rank : (k + 1) * rank, :] = up_ref[...]
    result = f32_dot(wide[...], ups[...]).astype(jnp.bfloat16)
    own_ref[...] = result[:tokens]
    for i, far_ref in enumerate(far_refs):

        @pl.when(pl.program_id(0) * len(far_refs) // KEY_VALUE_HEADS == i)
        def _(far_ref=far_ref):
            far_ref[...] = result[tokens:]


def expand(me, shrunk, far_shrunk, kv, ups, packed):
    tokens = shrunk.shape[0]
    marks = tuple(sorted(ups))
    rank, width = ups[0].shape
    block = width // KEY_VALUE_HEADS
    per = KEY_VALUE_HEADS // FAR_PARTS
    whole = [pl.BlockSpec(a.shape, lambda g: (0, 0)) for a in (shrunk, shrunk, kv)]
    return pl.pallas_call(
        functools.partial(expand_kernel, marks),
        grid=(KEY_VALUE_HEADS,),
        in_specs=[pl.BlockSpec(memory_space=pltpu.SMEM), *whole]
        + [pl.BlockSpec((rank, block), lambda g: (0, g))] * len(marks),
        out_specs=[
            pl.BlockSpec((tokens, block), lambda g: (0, g)),
            pl.BlockSpec((tokens, packed), lambda g: (0, 0)),
            pl.BlockSpec(kv.shape, lambda g: (0, 0)),
        ]
        + [
            pl.BlockSpec((packed, block), lambda g, i=i: (0, jnp.clip(g - i * per, 0, per - 1)))
            for i in range(FAR_PARTS)
        ],
        out_shape=[
            jax.ShapeDtypeStruct((tokens, width), jnp.bfloat16),
            jax.ShapeDtypeStruct((tokens, packed), jnp.bfloat16),
            jax.ShapeDtypeStruct(kv.shape, kv.dtype),
        ]
        + [jax.ShapeDtypeStruct((packed, per * block), jnp.bfloat16)] * FAR_PARTS,
        scratch_shapes=[
            pltpu.VMEM((tokens + packed, len(marks) * rank), jnp.bfloat16),
            pltpu.VMEM((len(marks) * rank, block), jnp.bfloat16),
        ],
        compiler_params=params(),
        cost_estimate=cost(16 * tokens * len(marks) * rank * width, 4 * tokens * width),
        name="expand",
    )(me, shrunk, far_shrunk, kv, *(ups[k] for k in marks))


def token_kernel(*refs):
    refs[-1][...] = jnp.zeros_like(refs[-1])


def token(*others):
    return pl.pallas_call(
        token_kernel,
        in_specs=[pl.BlockSpec(memory_space=pl.ANY)] * len(others),
        out_specs=pl.BlockSpec(memory_space=pltpu.VMEM),
        out_shape=jax.ShapeDtypeStruct((SUBLANES, 128), jnp.float32),
        compiler_params=params(),
        name="token",
    )(*others)


def hold(rows, *others):
    anywhere = pl.BlockSpec(memory_space=pl.ANY)
    return pl.pallas_call(
        lambda *refs: None,
        in_specs=[anywhere] + [pl.BlockSpec(memory_space=pltpu.HBM)] * len(others),
        out_specs=anywhere,
        out_shape=jax.ShapeDtypeStruct(rows.shape, rows.dtype),
        input_output_aliases={0: 0},
        compiler_params=params(),
        name="hold",
    )(rows, *others)


def swap_pairs(devices, distance):
    return [(i, i ^ distance) for i in range(devices)]


def mirrored(rows, devices):
    return lax.ppermute(rows, "seq", swap_pairs(devices, devices // 2))


def crossed(factors, devices):
    if lax.axis_size("groups") != 2:
        return mirrored(factors, devices)
    half = factors.shape[1] // 2
    return mirrored(jnp.where(lax.axis_index("groups") == 0, factors[:, :half], factors[:, half:]), devices)


def gathered_factors(factors, here, devices):
    if here.shape != factors.shape:
        first = lax.axis_index("groups") == 0
        there = lax.ppermute(here, "groups", [(0, 1), (1, 0)])
        here = jnp.concatenate([jnp.where(first, here, there), jnp.where(first, there, here)], axis=1)
    held = {0: factors, devices // 2: here}
    bit = devices // 4
    while bit:
        if bit != PLANE:
            swap = swap_pairs(devices, bit)
            held.update({k ^ bit: lax.ppermute(a, "seq", swap) for k, a in list(held.items())})
        bit //= 2
    return held


def window_chunks(kv, devices, reach):
    chunks = [(0, 0, kv)]
    for back in range(1, reach // PLANE + 1):
        hop = back * PLANE
        chunks.append((back, 0, lax.ppermute(kv, "seq", [(i, i + hop) for i in range(devices - hop)])))
    bit = PLANE // 2
    while bit:
        swap = swap_pairs(devices, bit)
        chunks = chunks + [(back, mark ^ bit, lax.ppermute(rows, "seq", swap)) for back, mark, rows in chunks]
        bit //= 2
    return chunks


def attend_kernel(reach, tags, parts, per, *refs):
    me_ref, request_ref, sq_ref, own_ref, unpack_ref = refs[:5]
    far_refs, refs = refs[5 : 5 + parts], refs[5 + parts :]
    chunk_refs = [(refs[2 * i], refs[2 * i + 1]) for i in range(len(tags))]
    out_ref, bias, keys, values, query, scores = refs[-6:]
    head = pl.program_id(0)
    me = me_ref[0]
    tokens = sq_ref.shape[0]
    for i, far_ref in enumerate(far_refs):

        @pl.when(head // per == i)
        def _(far_ref=far_ref):
            correction = own_ref[...].astype(jnp.float32) + f32_dot(unpack_ref[...], far_ref[...])
            query[...] = (sq_ref[...].astype(jnp.float32) + correction).astype(jnp.bfloat16)

    @pl.when(head == 0)
    def _():
        rows, lanes = row_iota((tokens, tokens)), lane_iota((tokens, tokens))
        own = request_ref[pl.ds(me, 1), :].astype(jnp.float32)
        own = jnp.sum(jnp.where(rows == lanes, own, 0.0), axis=1, keepdims=True)
        for at in range(reach + 1):
            source = me - reach + at
            theirs = request_ref[pl.ds(jnp.maximum(source, 0), 1), :].astype(jnp.float32)
            theirs = jnp.where(source >= 0, theirs, -1.0)
            allowed = own == theirs
            if at == reach:
                allowed = allowed & (lanes <= rows)
            bias[:, at * tokens : (at + 1) * tokens] = jnp.where(allowed, 0.0, -1e30)
        values[:, HEAD_SIZE:] = jnp.ones((values.shape[0], HEAD_SIZE), jnp.bfloat16)

    zeros = jnp.zeros((tokens, HEAD_SIZE), jnp.bfloat16)
    for at in range(reach):

        @pl.when(me - reach + at < 0)
        def _(at=at):
            keys[at * tokens : (at + 1) * tokens, :] = zeros
            values[at * tokens : (at + 1) * tokens, :HEAD_SIZE] = zeros

    for (back, mark), (k_ref, v_ref) in zip(tags, chunk_refs):
        source = (me // PLANE - back) * PLANE + jnp.bitwise_xor(me % PLANE, mark)
        at = source - me + reach

        @pl.when((source >= 0) & (at >= 0) & (at <= reach))
        def _(at=at, k_ref=k_ref, v_ref=v_ref):
            place = pl.ds(pl.multiple_of(at * tokens, tokens), tokens)
            keys[place, :] = k_ref[...]
            values[place, :HEAD_SIZE] = v_ref[...]

    factor = math.log2(math.e) / math.sqrt(HEAD_SIZE)
    heads = query.shape[1] // HEAD_SIZE

    def score(j):
        scores[j % 2] = lax.dot_general(
            query[:, j * HEAD_SIZE : (j + 1) * HEAD_SIZE],
            keys[...],
            (((1,), (1,)), ((), ())),
            preferred_element_type=jnp.float32,
        )

    score(0)
    for j in range(heads):
        if j + 1 < heads:
            score(j + 1)
        masked = scores[j % 2] + bias[...]
        raised = jnp.exp2((masked - jnp.max(masked, axis=1, keepdims=True)) * factor)
        blended = f32_dot(raised.astype(jnp.bfloat16), values[...])
        out_ref[:, j * HEAD_SIZE : (j + 1) * HEAD_SIZE] = (
            blended[:, :HEAD_SIZE] / blended[:, HEAD_SIZE:]
        ).astype(jnp.bfloat16)


def attend(me, requests, shared_query, own, unpack, far, chunks, reach, first, into=None):
    tokens, query_width = shared_query.shape
    block = query_width // KEY_VALUE_HEADS
    per = far[0].shape[1] // block
    heads = len(far) * per
    columns = pl.BlockSpec((tokens, block), lambda g: (0, first + g))
    in_specs = [
        pl.BlockSpec(memory_space=pltpu.SMEM),
        pl.BlockSpec(requests.shape, lambda g: (0, 0)),
        columns,
        columns,
        pl.BlockSpec(unpack.shape, lambda g: (0, 0)),
    ] + [pl.BlockSpec((a.shape[0], block), lambda g: (0, g % per)) for a in far]
    operands = [me, requests, shared_query, own, unpack, *far]
    for _, _, rows in chunks:
        in_specs.append(pl.BlockSpec((tokens, HEAD_SIZE), lambda g: (0, first + g)))
        in_specs.append(pl.BlockSpec((tokens, HEAD_SIZE), lambda g: (0, KEY_VALUE_HEADS + first + g)))
        operands += [rows, rows]
    aliases = {}
    if into is not None:
        aliases = {len(operands): 0}
        in_specs.append(pl.BlockSpec(memory_space=pl.ANY))
        operands.append(into)
    window = (reach + 1) * tokens
    return pl.pallas_call(
        functools.partial(attend_kernel, reach, tuple((b, m) for b, m, _ in chunks), len(far), per),
        grid=(heads,),
        in_specs=in_specs,
        out_specs=columns,
        out_shape=jax.ShapeDtypeStruct((tokens, query_width), jnp.bfloat16),
        scratch_shapes=[
            pltpu.VMEM((tokens, window), jnp.float32),
            pltpu.VMEM((window, HEAD_SIZE), jnp.bfloat16),
            pltpu.VMEM((window, 2 * HEAD_SIZE), jnp.bfloat16),
            pltpu.VMEM((tokens, block), jnp.bfloat16),
            pltpu.VMEM((2, tokens, window), jnp.float32),
        ],
        input_output_aliases=aliases,
        compiler_params=params(60),
        cost_estimate=cost(16 * heads * tokens * block * window, 8 * heads * tokens * block),
        name="attend",
    )(*operands)


def exchange(rows, devices):
    width = rows.shape[1]
    out = lax.all_to_all(
        rows.reshape(devices, rows.shape[0] // devices, width), "seq", split_axis=0, concat_axis=0, tiled=True
    )
    return out.reshape(rows.shape)


def local(
    normed,
    shared_query_rows,
    shared_key_rows,
    shared_value_rows,
    token_adapter,
    adapter_slot_table,
    adapter_down_factors,
    adapter_up_query,
    adapter_up_key_value,
    token_request,
):
    tokens = normed.shape[0]
    devices = lax.axis_size("seq")
    reach = devices // 2
    most = max(2, 3 * tokens // (2 * devices))
    fours = -(-most // 4)
    full, fold = fours // 2, fours % 2

    me = lax.axis_index("seq").astype(jnp.int32).reshape(1)
    factors = adapter_up_query[0]
    rank = factors.shape[0]
    here = crossed(factors, devices)
    outgoing, ids = dispatch(normed, token_adapter, adapter_slot_table, full, fold)
    incoming = exchange(hold(outgoing, here), devices)
    ups = gathered_factors(factors, here, devices)
    early = [token(*(ups[k] for k in ups if k))]
    back = exchange(project(incoming, adapter_down_factors, adapter_up_key_value, full, fold, *early), devices)
    kv, shrunk = correct(ids, back, shared_key_rows, shared_value_rows, rank, full, fold)
    swap = swap_pairs(devices, PLANE)
    packed = min(tokens, -(-devices // 2 * most // 16) * 16)
    far_shrunk = lax.ppermute(shrunk, "seq", swap)
    own, unpack, pages, *far = expand(me, shrunk, far_shrunk, kv, ups, packed)
    chunks = window_chunks(kv, devices, reach)
    pages = exchange(pages, devices)
    far = [lax.ppermute(a, "seq", swap) for a in far]
    requests = token_request.reshape(devices, tokens)
    attention = None
    for i in range(ATTEND_CALLS):
        some = far[i * FAR_PARTS // ATTEND_CALLS : (i + 1) * FAR_PARTS // ATTEND_CALLS]
        first = i * KEY_VALUE_HEADS // ATTEND_CALLS
        attention = attend(me, requests, shared_query_rows, own, unpack, some, chunks, reach, first, attention)
    width = pages.shape[1] // 2
    return (attention, pages[:, :width], pages[:, width:])


def solution(mesh):
    rows = P(("groups", "seq"), None)
    return jax.shard_map(
        local,
        mesh=mesh,
        in_specs=(
            rows,
            rows,
            rows,
            rows,
            rows,
            P(),
            P("seq", None, None),
            P("seq", None, None),
            P("seq", None, None, None),
            P("groups"),
        ),
        out_specs=(rows, rows, rows),
        check_vma=False,
    )
```

```python
import functools
import math

import jax
import jax.numpy as jnp
from jax import lax
from jax.experimental import pallas as pl
from jax.experimental.pallas import tpu as pltpu
from jax.sharding import PartitionSpec as P

KEY_VALUE_HEADS = 4
HEAD_SIZE = 128
SUBLANES = 8
PLANE = 4
MIB = 1024 * 1024


def params(mib=40):
    return pltpu.CompilerParams(vmem_limit_bytes=mib * MIB)


def cost(flops, moved):
    return pl.CostEstimate(flops=flops, bytes_accessed=moved, transcendentals=0)


def f32_dot(a, b):
    return jnp.dot(a, b, preferred_element_type=jnp.float32)


def lane_iota(shape):
    return lax.broadcasted_iota(jnp.int32, shape, 1)


def row_iota(shape):
    return lax.broadcasted_iota(jnp.int32, shape, 0)


def place_tokens(as_row, table_ref, stores):
    count = as_row.shape[1]
    rows, lanes = row_iota((count, count)), lane_iota((count, count))
    adapter = jnp.sum(jnp.where(rows == lanes, as_row, 0.0), axis=1, keepdims=True)
    same = adapter == as_row
    place_col = jnp.sum(jnp.where(same & (lanes < rows), 1.0, 0.0), axis=1, keepdims=True)
    place_row = jnp.sum(jnp.where(same & (rows < lanes), 1.0, 0.0), axis=0, keepdims=True)

    def owner(ids):
        result = jnp.zeros_like(ids)
        for k in range(stores):
            result = jnp.where(ids == float(k), table_ref[k].astype(jnp.float32), result)
        return result

    out = []
    for ids, place in ((adapter, place_col), (as_row, place_row)):
        block = jnp.floor(place * (1.0 / SUBLANES))
        out.append((owner(ids) * SUBLANES + place - block * SUBLANES, block))
    return out


def dispatch_kernel(full, fold, per_width, stores, adapter_ref, table_ref, a_ref, b_ref, x_ref, ids_ref, row_scr):
    step = pl.program_id(0)
    tokens = adapter_ref.shape[1]
    rows = x_ref.shape[0]

    @pl.when(step == 0)
    def _():
        cols, lanes = place_tokens(adapter_ref[...].astype(jnp.float32), table_ref, stores)
        lane = lane_iota((tokens, 128))
        ids_ref[...] = jnp.where(lane == 0, cols[0], jnp.where(lane == 1, cols[1], 0.0)).astype(jnp.int32)
        row_scr[0:1, :] = lanes[0]
        row_scr[1:2, :] = lanes[1]

    at = row_scr[0:1, :].astype(jnp.int32)
    block = row_scr[1:2, :].astype(jnp.int32)
    target = row_iota((rows, tokens))

    if full:

        @pl.when(step < full * per_width)
        def _():
            pick = ((at == target) & (block == step // per_width)).astype(jnp.bfloat16)
            x_ref[...] = f32_dot(pick, a_ref[...]).astype(jnp.bfloat16)

    if fold:

        @pl.when(step >= full * per_width)
        def _():
            low = ((at == target) & (block == full)).astype(jnp.bfloat16)
            high = ((at + 4 == target) & (block == full)).astype(jnp.bfloat16)
            x_ref[...] = (f32_dot(low, a_ref[...]) + f32_dot(high, b_ref[...])).astype(jnp.bfloat16)


def dispatch(normed, token_adapter, table, full, fold):
    tokens, width = normed.shape
    stores = table.shape[0]
    column = width // 4
    per_width, half = width // column, width // 2 // column
    steps = full * per_width + fold * half

    def a_map(i):
        return (0, jnp.where(i < full * per_width, i % per_width, i - full * per_width))

    def b_map(i):
        return (0, jnp.where(i < full * per_width, half, i - full * per_width + half))

    return pl.pallas_call(
        functools.partial(dispatch_kernel, full, fold, per_width, stores),
        grid=(steps,),
        in_specs=[
            pl.BlockSpec((1, tokens), lambda i: (0, 0)),
            pl.BlockSpec(memory_space=pltpu.SMEM),
            pl.BlockSpec((tokens, column), a_map),
            pl.BlockSpec((tokens, column), b_map),
        ],
        out_specs=[
            pl.BlockSpec((stores * SUBLANES, column), lambda i: (0, i)),
            pl.BlockSpec((tokens, 128), lambda i: (0, 0)),
        ],
        out_shape=[
            jax.ShapeDtypeStruct((stores * SUBLANES, steps * column), jnp.bfloat16),
            jax.ShapeDtypeStruct((tokens, 128), jnp.int32),
        ],
        scratch_shapes=[pltpu.VMEM((8, tokens), jnp.float32)],
        compiler_params=params(),
        name="dispatch",
    )(token_adapter.reshape(1, tokens), table, normed, normed)


def project_kernel(full, fold, steps, *refs):
    refs = list(refs)
    low_refs = [(refs.pop(0), refs.pop(0)) for _ in range(full)]
    fold_ref = refs.pop(0) if fold else None
    (down_low, down_high, up_kv), (out_ref, acc) = refs[:3], refs[-2:]
    step = pl.program_id(0)
    rank = up_kv.shape[2]

    @pl.when(step == 0)
    def _():
        acc[...] = jnp.zeros_like(acc)

    low, high = down_low[0], down_high[0]
    for b, (x_low, x_high) in enumerate(low_refs):
        acc[b] += f32_dot(x_low[...], low) + f32_dot(x_high[...], high)
    if fold:
        acc[full] += f32_dot(fold_ref[...], low)
        acc[full + 1] += f32_dot(fold_ref[...], high)

    @pl.when(step == steps - 1)
    def _():
        kv_width = up_kv.shape[3]
        queries = []
        for b in range(full):
            shrunk = acc[b].astype(jnp.bfloat16)
            at = b * 2 * kv_width
            for i in range(2):
                piece = shrunk[:, (i + 1) * rank : (i + 2) * rank]
                out_ref[:, at + i * kv_width : at + (i + 1) * kv_width] = f32_dot(piece, up_kv[0, i]).astype(jnp.bfloat16)
            queries.append(shrunk[:, :rank])
        if fold:
            rows = acc.shape[1]
            upper = (row_iota((rows, 1)) % SUBLANES) >= 4
            mixed = jnp.where(upper, acc[full + 1], acc[full]).reshape(rows // SUBLANES, SUBLANES, 3 * rank)
            both = mixed + jnp.concatenate([mixed[:, 4:], mixed[:, :4]], axis=1)
            shrunk = both.reshape(rows, 3 * rank).astype(jnp.bfloat16)
            delta = [f32_dot(shrunk[:, (i + 1) * rank : (i + 2) * rank], up_kv[0, i]) for i in range(2)]
            at = full * 2 * kv_width
            out_ref[:, at : at + kv_width] = jnp.where(upper, delta[1], delta[0]).astype(jnp.bfloat16)
            queries.append(shrunk[:, :rank])
        if len(queries) % 2:
            queries.append(jnp.zeros_like(queries[0]))
        out_ref[:, (2 * full + fold) * kv_width :] = jnp.concatenate(queries, axis=1)


def project(x, down, up_kv, full, fold, *others):
    rows = x.shape[0]
    _, width, ranks = down.shape
    column = width // 8
    steps = width // 2 // column
    _, _, rank, kv_width = up_kv.shape
    in_specs = []
    for b in range(full):
        in_specs.append(pl.BlockSpec((rows, column), lambda i, b=b: (0, 2 * b * steps + i)))
        in_specs.append(pl.BlockSpec((rows, column), lambda i, b=b: (0, (2 * b + 1) * steps + i)))
    if fold:
        in_specs.append(pl.BlockSpec((rows, column), lambda i: (0, 2 * full * steps + i)))
    blocks = len(in_specs)
    in_specs += [
        pl.BlockSpec((1, column, ranks), lambda i: (0, i, 0)),
        pl.BlockSpec((1, column, ranks), lambda i: (0, steps + i, 0)),
        pl.BlockSpec(up_kv.shape, lambda i: (0, 0, 0, 0)),
    ]
    in_specs += [pl.BlockSpec(memory_space=pltpu.HBM)] * len(others)
    shape = (rows, (2 * full + fold) * kv_width + (full + fold + 1) // 2 * 2 * rank)
    return pl.pallas_call(
        functools.partial(project_kernel, full, fold, steps),
        grid=(steps,),
        in_specs=in_specs,
        out_specs=pl.BlockSpec(shape, lambda i: (0, 0)),
        out_shape=jax.ShapeDtypeStruct(shape, jnp.bfloat16),
        scratch_shapes=[pltpu.VMEM((full + 2 * fold, rows, ranks), jnp.float32)],
        compiler_params=params(),
        name="project",
    )(*([x] * blocks), down, down, up_kv, *others)


def picks(at, chosen, rows):
    return ((at == lane_iota((at.shape[0], rows))) & chosen).astype(jnp.bfloat16)


def correct_kernel(full, fold, rank, ids_ref, back_ref, sk_ref, sv_ref, kv_ref, shrunk_ref):
    rows = back_ref.shape[0]
    width = sk_ref.shape[1]
    place, block = ids_ref[:, 0:1], ids_ref[:, 1:2]
    queries = (2 * full + fold) * width
    total = [0.0, 0.0, 0.0]
    for b in range(full + fold):
        pick = picks(place, block == b, rows)
        for i in range(2):
            if b < full:
                at = (2 * b + i) * width
            else:
                at = 2 * full * width
                pick = pick if i == 0 else picks(place + 4, block == b, rows)
            total[i] += f32_dot(pick, back_ref[:, at : at + width])
    for b in range(full + fold):
        at = queries + b // 2 * 2 * rank
        both = f32_dot(picks(place, block == b, rows), back_ref[:, at : at + 2 * rank])
        total[2] += both if b % 2 == 0 else pltpu.roll(both, rank, 1)
    kv_ref[:, :width] = (sk_ref[...].astype(jnp.float32) + total[0]).astype(jnp.bfloat16)
    kv_ref[:, width:] = (sv_ref[...].astype(jnp.float32) + total[1]).astype(jnp.bfloat16)
    lanes = lane_iota(shrunk_ref.shape)
    owner = (place // SUBLANES).astype(jnp.float32)
    shrunk_ref[...] = jnp.where(lanes < rank, total[2], jnp.where(lanes == rank, owner, 0.0)).astype(jnp.bfloat16)


def correct(ids, back, shared_keys, shared_values, rank, full, fold):
    rows, width = shared_keys.shape
    return pl.pallas_call(
        functools.partial(correct_kernel, full, fold, rank),
        out_shape=[
            jax.ShapeDtypeStruct((rows, 2 * width), jnp.bfloat16),
            jax.ShapeDtypeStruct((rows, 2 * rank), jnp.bfloat16),
        ],
        compiler_params=params(),
        name="correct",
    )(ids, back, shared_keys, shared_values)


def packing(owner, me, rows):
    tokens = owner.shape[0]
    held = jnp.bitwise_and(jnp.bitwise_xor(owner, me), PLANE) == 0
    flags = jnp.broadcast_to(held.astype(jnp.float32), (tokens, tokens)).astype(jnp.bfloat16)
    before = (lane_iota((tokens, tokens)) < row_iota((tokens, tokens))).astype(jnp.bfloat16)
    place = f32_dot(before, flags)[:, :1].astype(jnp.int32)
    return ((place == lane_iota((tokens, rows))) & held).astype(jnp.bfloat16)


def expand_kernel(marks, me_ref, own_rows_ref, far_rows_ref, kv_ref, sq_ref, *refs):
    up_refs, refs = refs[: len(marks)], refs[len(marks) :]
    query_ref, unpack_ref, pages_ref, far_ref, wide, ups, held, sems = refs
    tokens, packed = unpack_ref.shape
    parts, _, block = held.shape
    rank = up_refs[0].shape[0]
    me = me_ref[0]

    def fetches(g):
        columns = slice(g * block, (g + 1) * block)
        yield pltpu.make_async_copy(sq_ref.at[:, columns], held.at[g], sems.at[g, len(marks)])
        for k, up_ref in enumerate(up_refs):
            place = ups.at[g, k * rank : (k + 1) * rank, :]
            yield pltpu.make_async_copy(up_ref.at[:, columns], place, sems.at[g, k])

    for g in range(parts):
        for copy in fetches(g):
            copy.start()

    pages_ref[...] = kv_ref[...]

    def owners(rows):
        return rows[:, rank : rank + 1].astype(jnp.float32).astype(jnp.int32)

    def widen(rows, owner, at):
        count = rows.shape[0]
        lanes = lane_iota((count, 2 * rank))
        apart = jnp.bitwise_xor(owner, me)
        twice = jnp.where(lanes < rank, rows, pltpu.roll(rows, rank, 1))
        for k in range(0, len(marks), 2):
            wanted = jnp.where(lanes < rank, marks[k], marks[k + 1])
            kept = jnp.where(apart == wanted, twice, 0.0).astype(jnp.bfloat16)
            wide[at : at + count, k * rank : (k + 2) * rank] = kept

    own_rows, far_rows = own_rows_ref[...], far_rows_ref[...]
    own_owner = owners(own_rows)
    unpack_ref[...] = packing(own_owner, jnp.bitwise_xor(me, PLANE), packed)
    widen(own_rows.astype(jnp.float32), own_owner, 0)
    pack = packing(owners(far_rows), me, packed)
    far_rows = lax.dot_general(pack, far_rows, (((0,), (0,)), ((), ())), preferred_element_type=jnp.float32)
    widen(far_rows, owners(far_rows), tokens)

    for g in range(parts):
        for copy in fetches(g):
            copy.wait()
        columns = slice(g * block, (g + 1) * block)
        result = f32_dot(wide[...], ups[g]).astype(jnp.bfloat16)
        own = result[:tokens].astype(jnp.float32)
        query_ref[:, columns] = (held[g].astype(jnp.float32) + own).astype(jnp.bfloat16)
        far_ref[:, columns] = result[tokens:]


def expand(me, shrunk, far_shrunk, kv, shared_query, ups, packed):
    tokens = shrunk.shape[0]
    marks = tuple(sorted(ups))
    rank, width = ups[0].shape
    block = width // KEY_VALUE_HEADS
    vmem, anywhere = pl.BlockSpec(memory_space=pltpu.VMEM), pl.BlockSpec(memory_space=pl.ANY)
    return pl.pallas_call(
        functools.partial(expand_kernel, marks),
        in_specs=[pl.BlockSpec(memory_space=pltpu.SMEM)] + [vmem] * 3 + [anywhere] * (1 + len(marks)),
        out_specs=[vmem] * 4,
        out_shape=[
            jax.ShapeDtypeStruct(shape, jnp.bfloat16)
            for shape in ((tokens, width), (tokens, packed), kv.shape, (packed, width))
        ],
        scratch_shapes=[
            pltpu.VMEM((tokens + packed, len(marks) * rank), jnp.bfloat16),
            pltpu.VMEM((KEY_VALUE_HEADS, len(marks) * rank, block), jnp.bfloat16),
            pltpu.VMEM((KEY_VALUE_HEADS, tokens, block), jnp.bfloat16),
            pltpu.SemaphoreType.DMA((KEY_VALUE_HEADS, len(marks) + 1)),
        ],
        compiler_params=params(60),
        cost_estimate=cost(16 * tokens * len(marks) * rank * width, 4 * tokens * width),
        name="expand",
    )(me, shrunk, far_shrunk, kv, shared_query, *(ups[k] for k in marks))


def token_kernel(*refs):
    refs[-1][...] = jnp.zeros_like(refs[-1])


def token(*others):
    return pl.pallas_call(
        token_kernel,
        in_specs=[pl.BlockSpec(memory_space=pl.ANY)] * len(others),
        out_specs=pl.BlockSpec(memory_space=pltpu.VMEM),
        out_shape=jax.ShapeDtypeStruct((SUBLANES, 128), jnp.float32),
        compiler_params=params(),
        name="token",
    )(*others)


def hold(rows, *others):
    anywhere = pl.BlockSpec(memory_space=pl.ANY)
    return pl.pallas_call(
        lambda *refs: None,
        in_specs=[anywhere] + [pl.BlockSpec(memory_space=pltpu.HBM)] * len(others),
        out_specs=anywhere,
        out_shape=jax.ShapeDtypeStruct(rows.shape, rows.dtype),
        input_output_aliases={0: 0},
        compiler_params=params(60),
        name="hold",
    )(rows, *others)


def swap_pairs(devices, distance):
    return [(i, i ^ distance) for i in range(devices)]


def mirrored(rows, devices):
    return lax.ppermute(rows, "seq", swap_pairs(devices, devices // 2))


def crossed(factors, devices):
    if lax.axis_size("groups") != 2:
        return mirrored(factors, devices)
    half = factors.shape[1] // 2
    return mirrored(jnp.where(lax.axis_index("groups") == 0, factors[:, :half], factors[:, half:]), devices)


def gathered_factors(factors, here, devices):
    if here.shape != factors.shape:
        first = lax.axis_index("groups") == 0
        there = lax.ppermute(here, "groups", [(0, 1), (1, 0)])
        here = jnp.concatenate([jnp.where(first, here, there), jnp.where(first, there, here)], axis=1)
    held = {0: factors, devices // 2: here}
    bit = devices // 4
    while bit:
        if bit != PLANE:
            swap = swap_pairs(devices, bit)
            held.update({k ^ bit: lax.ppermute(a, "seq", swap) for k, a in list(held.items())})
        bit //= 2
    return held


def window_chunks(kv, devices, reach):
    chunks = [(0, 0, kv)]
    for back in range(1, reach // PLANE + 1):
        hop = back * PLANE
        chunks.append((back, 0, lax.ppermute(kv, "seq", [(i, i + hop) for i in range(devices - hop)])))
    bit = PLANE // 2
    while bit:
        swap = swap_pairs(devices, bit)
        chunks = chunks + [(back, mark ^ bit, lax.ppermute(rows, "seq", swap)) for back, mark, rows in chunks]
        bit //= 2
    return chunks


def attend_kernel(reach, tags, width, me_ref, request_ref, query_ref, unpack_ref, far_ref, *refs):
    chunk_refs, refs = refs[: len(tags)], refs[len(tags) :]
    out_ref, window, keys, values, query, scores, held, far_held, done, sems = refs
    me = me_ref[0]
    parts, tokens, block = held.shape
    heads = block // HEAD_SIZE
    last = len(tags)

    def chunk_fetch(c):
        back, mark = tags[c]
        source = (me // PLANE - back) * PLANE + jnp.bitwise_xor(me % PLANE, mark)
        at = source - me + reach
        place = pl.ds(pl.multiple_of(at * tokens, tokens), tokens)
        copy = pltpu.make_async_copy(chunk_refs[c], window.at[place, :], sems.at[c])
        return (source >= 0) & (at >= 0) & (at <= reach), copy

    def columns(g):
        return pl.ds(pl.multiple_of(g * block, block), block)

    def query_fetches(g):
        return [
            pltpu.make_async_copy(query_ref.at[:, columns(g)], held.at[g], sems.at[last + g]),
            pltpu.make_async_copy(far_ref.at[:, columns(g)], far_held.at[g], sems.at[last + parts + g]),
        ]

    def store(g):
        return pltpu.make_async_copy(done.at[g], out_ref.at[:, columns(g)], sems.at[last + 2 * parts + g])

    for copy in query_fetches(0):
        copy.start()
    for c in range(len(tags)):
        wanted, copy = chunk_fetch(c)
        pl.when(wanted)(copy.start)
    for g in range(1, parts):
        for copy in query_fetches(g):
            copy.start()

    rows, lanes = row_iota((tokens, tokens)), lane_iota((tokens, tokens))
    own = request_ref[pl.ds(me, 1), :].astype(jnp.float32)
    for at in range(reach + 1):
        source = me - reach + at
        span = slice(at * tokens, (at + 1) * tokens)
        theirs = request_ref[pl.ds(jnp.maximum(source, 0), 1), :].astype(jnp.float32)
        theirs = jnp.sum(jnp.where(rows == lanes, theirs, 0.0), axis=1, keepdims=True)
        allowed = jnp.where(source >= 0, theirs, -1.0) == own
        if at == reach:
            allowed = allowed & (rows <= lanes)
        keys[span, HEAD_SIZE:] = jnp.where(allowed, 0.0, -1e30).astype(jnp.bfloat16)

        @pl.when(source < 0)
        def _(span=span):
            window[span, :] = jnp.zeros((tokens, 2 * width), jnp.bfloat16)

    values[:, HEAD_SIZE:] = jnp.ones((values.shape[0], HEAD_SIZE), jnp.bfloat16)
    for j in range(heads):
        query[j, :, HEAD_SIZE:] = (rows == lanes).astype(jnp.bfloat16)
    factor = math.log2(math.e) / math.sqrt(HEAD_SIZE)
    for c in range(len(tags)):
        wanted, copy = chunk_fetch(c)
        pl.when(wanted)(copy.wait)

    @pl.loop(0, parts)
    def _(g):
        for copy in query_fetches(g):
            copy.wait()
        correction = f32_dot(unpack_ref[...], far_held[g])
        corrected = (held[g].astype(jnp.float32) + correction).astype(jnp.bfloat16)
        for j in range(heads):
            query[j, :, 0:HEAD_SIZE] = corrected[:, j * HEAD_SIZE : (j + 1) * HEAD_SIZE]
        at = pl.multiple_of(g * HEAD_SIZE, HEAD_SIZE)
        keys[:, 0:HEAD_SIZE] = window[:, pl.ds(at, HEAD_SIZE)]
        values[:, 0:HEAD_SIZE] = window[:, pl.ds(pl.multiple_of(width + at, HEAD_SIZE), HEAD_SIZE)]

        def score(j):
            stacked = query[4 * j : 4 * j + 4].reshape(4 * tokens, HEAD_SIZE + tokens)
            scores[j % 2] = lax.dot_general(
                stacked, keys[...], (((1,), (1,)), ((), ())), preferred_element_type=jnp.float32
            )

        score(0)
        for j in range(heads // 4):
            if j + 1 < heads // 4:
                score(j + 1)
            for k in range(2):
                masked = scores[j % 2, 2 * k * tokens : 2 * (k + 1) * tokens]
                raised = jnp.exp2((masked - jnp.max(masked, axis=1, keepdims=True)) * factor)
                blended = f32_dot(raised.astype(jnp.bfloat16), values[...])
                for i in range(2):
                    head = 4 * j + 2 * k + i
                    part = blended[i * tokens : (i + 1) * tokens]
                    result = part[:, :HEAD_SIZE] / part[:, HEAD_SIZE:]
                    done[g, :, head * HEAD_SIZE : (head + 1) * HEAD_SIZE] = result.astype(jnp.bfloat16)
        store(g).start()

    for g in range(parts):
        store(g).wait()


def attend(me, requests, query, unpack, far, chunks, reach):
    tokens, query_width = query.shape
    block = query_width // KEY_VALUE_HEADS
    length = (reach + 1) * tokens
    width = chunks[0][2].shape[1] // 2
    vmem, anywhere = pl.BlockSpec(memory_space=pltpu.VMEM), pl.BlockSpec(memory_space=pl.ANY)
    return pl.pallas_call(
        functools.partial(attend_kernel, reach, tuple((b, m) for b, m, _ in chunks), width),
        in_specs=[pl.BlockSpec(memory_space=pltpu.SMEM), vmem, anywhere, vmem] + [anywhere] * (1 + len(chunks)),
        out_specs=anywhere,
        out_shape=jax.ShapeDtypeStruct((tokens, query_width), jnp.bfloat16),
        scratch_shapes=[
            pltpu.VMEM((length, 2 * width), jnp.bfloat16),
            pltpu.VMEM((length, HEAD_SIZE + tokens), jnp.bfloat16),
            pltpu.VMEM((length, 2 * HEAD_SIZE), jnp.bfloat16),
            pltpu.VMEM((block // HEAD_SIZE, tokens, HEAD_SIZE + tokens), jnp.bfloat16),
            pltpu.VMEM((2, 4 * tokens, length), jnp.float32),
            pltpu.VMEM((KEY_VALUE_HEADS, tokens, block), jnp.bfloat16),
            pltpu.VMEM((KEY_VALUE_HEADS, far.shape[0], block), jnp.bfloat16),
            pltpu.VMEM((KEY_VALUE_HEADS, tokens, block), jnp.bfloat16),
            pltpu.SemaphoreType.DMA((len(chunks) + 3 * KEY_VALUE_HEADS,)),
        ],
        compiler_params=params(60),
        cost_estimate=cost(16 * tokens * query_width * length, 8 * tokens * query_width),
        name="attend",
    )(me, requests, query, unpack, far, *(rows for _, _, rows in chunks))


def exchange(rows, devices):
    width = rows.shape[1]
    out = lax.all_to_all(
        rows.reshape(devices, rows.shape[0] // devices, width), "seq", split_axis=0, concat_axis=0, tiled=True
    )
    return out.reshape(rows.shape)


def local(
    normed,
    shared_query_rows,
    shared_key_rows,
    shared_value_rows,
    token_adapter,
    adapter_slot_table,
    adapter_down_factors,
    adapter_up_query,
    adapter_up_key_value,
    token_request,
):
    tokens = normed.shape[0]
    devices = lax.axis_size("seq")
    reach = devices // 2
    most = max(2, 3 * tokens // (2 * devices))
    fours = -(-most // 4)
    full, fold = fours // 2, fours % 2

    me = lax.axis_index("seq").astype(jnp.int32).reshape(1)
    factors = adapter_up_query[0]
    rank = factors.shape[0]
    here = crossed(factors, devices)
    outgoing, ids = dispatch(normed, token_adapter, adapter_slot_table, full, fold)
    incoming = exchange(hold(outgoing, here), devices)
    ups = gathered_factors(factors, here, devices)
    early = [token(*(ups[k] for k in ups if k))]
    back = exchange(project(incoming, adapter_down_factors, adapter_up_key_value, full, fold, *early), devices)
    kv, shrunk = correct(ids, back, shared_key_rows, shared_value_rows, rank, full, fold)
    swap = swap_pairs(devices, PLANE)
    packed = min(tokens, -(-devices // 2 * most // 16) * 16)
    far_shrunk = lax.ppermute(shrunk, "seq", swap)
    query, unpack, pages, far = expand(me, shrunk, far_shrunk, kv, shared_query_rows, ups, packed)
    chunks = window_chunks(kv, devices, reach)
    pages = exchange(pages, devices)
    far = lax.ppermute(far, "seq", swap)
    requests = token_request.reshape(devices, tokens)
    attention = attend(me, requests, query, unpack, far, chunks, reach)
    width = pages.shape[1] // 2
    return (attention, pages[:, :width], pages[:, width:])


def solution(mesh):
    rows = P(("groups", "seq"), None)
    return jax.shard_map(
        local,
        mesh=mesh,
        in_specs=(
            rows,
            rows,
            rows,
            rows,
            rows,
            P(),
            P("seq", None, None),
            P("seq", None, None),
            P("seq", None, None, None),
            P("groups"),
        ),
        out_specs=(rows, rows, rows),
        check_vma=False,
    )
```

```python
import functools
import math

import jax
import jax.numpy as jnp
from jax import lax
from jax.experimental import pallas as pl
from jax.experimental.pallas import tpu as pltpu
from jax.sharding import PartitionSpec as P

KEY_VALUE_HEADS = 4
HEAD_SIZE = 128
SUBLANES = 8
PLANE = 4
MIB = 1024 * 1024


def params(mib=40):
    return pltpu.CompilerParams(vmem_limit_bytes=mib * MIB)


def cost(flops, moved):
    return pl.CostEstimate(flops=flops, bytes_accessed=moved, transcendentals=0)


def f32_dot(a, b):
    return jnp.dot(a, b, preferred_element_type=jnp.float32)


def lane_iota(shape):
    return lax.broadcasted_iota(jnp.int32, shape, 1)


def row_iota(shape):
    return lax.broadcasted_iota(jnp.int32, shape, 0)


def place_tokens(as_row, table_ref, stores):
    count = as_row.shape[1]
    rows, lanes = row_iota((count, count)), lane_iota((count, count))
    adapter = jnp.sum(jnp.where(rows == lanes, as_row, 0.0), axis=1, keepdims=True)
    same = adapter == as_row
    place_col = jnp.sum(jnp.where(same & (lanes < rows), 1.0, 0.0), axis=1, keepdims=True)
    place_row = jnp.sum(jnp.where(same & (rows < lanes), 1.0, 0.0), axis=0, keepdims=True)

    def owner(ids):
        result = jnp.zeros_like(ids)
        for k in range(stores):
            result = jnp.where(ids == float(k), table_ref[k].astype(jnp.float32), result)
        return result

    out = []
    for ids, place in ((adapter, place_col), (as_row, place_row)):
        block = jnp.floor(place * (1.0 / SUBLANES))
        out.append((owner(ids) * SUBLANES + place - block * SUBLANES, block))
    return out


def dispatch_kernel(full, fold, per_width, stores, adapter_ref, table_ref, a_ref, b_ref, x_ref, ids_ref, row_scr):
    step = pl.program_id(0)
    tokens = adapter_ref.shape[1]
    rows = x_ref.shape[0]

    @pl.when(step == 0)
    def _():
        cols, lanes = place_tokens(adapter_ref[...].astype(jnp.float32), table_ref, stores)
        lane = lane_iota((tokens, 128))
        ids_ref[...] = jnp.where(lane == 0, cols[0], jnp.where(lane == 1, cols[1], 0.0)).astype(jnp.int32)
        row_scr[0:1, :] = lanes[0]
        row_scr[1:2, :] = lanes[1]

    at = row_scr[0:1, :].astype(jnp.int32)
    block = row_scr[1:2, :].astype(jnp.int32)
    target = row_iota((rows, tokens))

    if full:

        @pl.when(step < full * per_width)
        def _():
            pick = ((at == target) & (block == step // per_width)).astype(jnp.bfloat16)
            x_ref[...] = f32_dot(pick, a_ref[...]).astype(jnp.bfloat16)

    if fold:

        @pl.when(step >= full * per_width)
        def _():
            low = ((at == target) & (block == full)).astype(jnp.bfloat16)
            high = ((at + 4 == target) & (block == full)).astype(jnp.bfloat16)
            x_ref[...] = (f32_dot(low, a_ref[...]) + f32_dot(high, b_ref[...])).astype(jnp.bfloat16)


def dispatch(normed, token_adapter, table, full, fold):
    tokens, width = normed.shape
    stores = table.shape[0]
    column = width // 4
    per_width, half = width // column, width // 2 // column
    steps = full * per_width + fold * half

    def a_map(i):
        return (0, jnp.where(i < full * per_width, i % per_width, i - full * per_width))

    def b_map(i):
        return (0, jnp.where(i < full * per_width, half, i - full * per_width + half))

    return pl.pallas_call(
        functools.partial(dispatch_kernel, full, fold, per_width, stores),
        grid=(steps,),
        in_specs=[
            pl.BlockSpec((1, tokens), lambda i: (0, 0)),
            pl.BlockSpec(memory_space=pltpu.SMEM),
            pl.BlockSpec((tokens, column), a_map),
            pl.BlockSpec((tokens, column), b_map),
        ],
        out_specs=[
            pl.BlockSpec((stores * SUBLANES, column), lambda i: (0, i)),
            pl.BlockSpec((tokens, 128), lambda i: (0, 0)),
        ],
        out_shape=[
            jax.ShapeDtypeStruct((stores * SUBLANES, steps * column), jnp.bfloat16),
            jax.ShapeDtypeStruct((tokens, 128), jnp.int32),
        ],
        scratch_shapes=[pltpu.VMEM((8, tokens), jnp.float32)],
        compiler_params=params(),
        name="dispatch",
    )(token_adapter.reshape(1, tokens), table, normed, normed)


def project_kernel(full, fold, steps, *refs):
    refs = list(refs)
    low_refs = [(refs.pop(0), refs.pop(0)) for _ in range(full)]
    fold_ref = refs.pop(0) if fold else None
    (down_low, down_high, up_kv), (out_ref, acc) = refs[:3], refs[-2:]
    step = pl.program_id(0)
    rank = up_kv.shape[2]

    @pl.when(step == 0)
    def _():
        acc[...] = jnp.zeros_like(acc)

    low, high = down_low[0], down_high[0]
    for b, (x_low, x_high) in enumerate(low_refs):
        acc[b] += f32_dot(x_low[...], low) + f32_dot(x_high[...], high)
    if fold:
        acc[full] += f32_dot(fold_ref[...], low)
        acc[full + 1] += f32_dot(fold_ref[...], high)

    @pl.when(step == steps - 1)
    def _():
        kv_width = up_kv.shape[3]
        queries = []
        for b in range(full):
            shrunk = acc[b].astype(jnp.bfloat16)
            at = b * 2 * kv_width
            for i in range(2):
                piece = shrunk[:, (i + 1) * rank : (i + 2) * rank]
                out_ref[:, at + i * kv_width : at + (i + 1) * kv_width] = f32_dot(piece, up_kv[0, i]).astype(jnp.bfloat16)
            queries.append(shrunk[:, :rank])
        if fold:
            rows = acc.shape[1]
            upper = (row_iota((rows, 1)) % SUBLANES) >= 4
            mixed = jnp.where(upper, acc[full + 1], acc[full]).reshape(rows // SUBLANES, SUBLANES, 3 * rank)
            both = mixed + jnp.concatenate([mixed[:, 4:], mixed[:, :4]], axis=1)
            shrunk = both.reshape(rows, 3 * rank).astype(jnp.bfloat16)
            delta = [f32_dot(shrunk[:, (i + 1) * rank : (i + 2) * rank], up_kv[0, i]) for i in range(2)]
            at = full * 2 * kv_width
            out_ref[:, at : at + kv_width] = jnp.where(upper, delta[1], delta[0]).astype(jnp.bfloat16)
            queries.append(shrunk[:, :rank])
        if len(queries) % 2:
            queries.append(jnp.zeros_like(queries[0]))
        out_ref[:, (2 * full + fold) * kv_width :] = jnp.concatenate(queries, axis=1)


def project(x, down, up_kv, full, fold, *others):
    rows = x.shape[0]
    _, width, ranks = down.shape
    column = width // 8
    steps = width // 2 // column
    _, _, rank, kv_width = up_kv.shape
    in_specs = []
    for b in range(full):
        in_specs.append(pl.BlockSpec((rows, column), lambda i, b=b: (0, 2 * b * steps + i)))
        in_specs.append(pl.BlockSpec((rows, column), lambda i, b=b: (0, (2 * b + 1) * steps + i)))
    if fold:
        in_specs.append(pl.BlockSpec((rows, column), lambda i: (0, 2 * full * steps + i)))
    blocks = len(in_specs)
    in_specs += [
        pl.BlockSpec((1, column, ranks), lambda i: (0, i, 0)),
        pl.BlockSpec((1, column, ranks), lambda i: (0, steps + i, 0)),
        pl.BlockSpec(up_kv.shape, lambda i: (0, 0, 0, 0)),
    ]
    in_specs += [pl.BlockSpec(memory_space=pltpu.HBM)] * len(others)
    shape = (rows, (2 * full + fold) * kv_width + (full + fold + 1) // 2 * 2 * rank)
    return pl.pallas_call(
        functools.partial(project_kernel, full, fold, steps),
        grid=(steps,),
        in_specs=in_specs,
        out_specs=pl.BlockSpec(shape, lambda i: (0, 0)),
        out_shape=jax.ShapeDtypeStruct(shape, jnp.bfloat16),
        scratch_shapes=[pltpu.VMEM((full + 2 * fold, rows, ranks), jnp.float32)],
        compiler_params=params(),
        name="project",
    )(*([x] * blocks), down, down, up_kv, *others)


def picks(at, chosen, rows):
    return ((at == lane_iota((at.shape[0], rows))) & chosen).astype(jnp.bfloat16)


def correct_kernel(full, fold, rank, ids_ref, back_ref, sk_ref, sv_ref, kv_ref, shrunk_ref):
    rows = back_ref.shape[0]
    width = sk_ref.shape[1]
    place, block = ids_ref[:, 0:1], ids_ref[:, 1:2]
    queries = (2 * full + fold) * width
    total = [0.0, 0.0, 0.0]
    for b in range(full + fold):
        pick = picks(place, block == b, rows)
        for i in range(2):
            if b < full:
                at = (2 * b + i) * width
            else:
                at = 2 * full * width
                pick = pick if i == 0 else picks(place + 4, block == b, rows)
            total[i] += f32_dot(pick, back_ref[:, at : at + width])
    for b in range(full + fold):
        at = queries + b // 2 * 2 * rank
        both = f32_dot(picks(place, block == b, rows), back_ref[:, at : at + 2 * rank])
        total[2] += both if b % 2 == 0 else pltpu.roll(both, rank, 1)
    kv_ref[:, :width] = (sk_ref[...].astype(jnp.float32) + total[0]).astype(jnp.bfloat16)
    kv_ref[:, width:] = (sv_ref[...].astype(jnp.float32) + total[1]).astype(jnp.bfloat16)
    lanes = lane_iota(shrunk_ref.shape)
    owner = (place // SUBLANES).astype(jnp.float32)
    shrunk_ref[...] = jnp.where(lanes < rank, total[2], jnp.where(lanes == rank, owner, 0.0)).astype(jnp.bfloat16)


def correct(ids, back, shared_keys, shared_values, rank, full, fold):
    rows, width = shared_keys.shape
    return pl.pallas_call(
        functools.partial(correct_kernel, full, fold, rank),
        out_shape=[
            jax.ShapeDtypeStruct((rows, 2 * width), jnp.bfloat16),
            jax.ShapeDtypeStruct((rows, 2 * rank), jnp.bfloat16),
        ],
        compiler_params=params(),
        name="correct",
    )(ids, back, shared_keys, shared_values)


def packing(owner, me, rows):
    tokens = owner.shape[0]
    held = jnp.bitwise_and(jnp.bitwise_xor(owner, me), PLANE) == 0
    flags = jnp.broadcast_to(held.astype(jnp.float32), (tokens, tokens)).astype(jnp.bfloat16)
    before = (lane_iota((tokens, tokens)) < row_iota((tokens, tokens))).astype(jnp.bfloat16)
    place = f32_dot(before, flags)[:, :1].astype(jnp.int32)
    return ((place == lane_iota((tokens, rows))) & held).astype(jnp.bfloat16)


def expand_kernel(marks, me_ref, own_rows_ref, far_rows_ref, kv_ref, sq_ref, *refs):
    up_refs, refs = refs[: len(marks)], refs[len(marks) :]
    query_ref, unpack_ref, pages_ref, far_ref, wide, ups, held, sems = refs
    tokens, packed = unpack_ref.shape
    parts, _, block = held.shape
    rank = up_refs[0].shape[0]
    me = me_ref[0]

    def fetches(g):
        columns = slice(g * block, (g + 1) * block)
        yield pltpu.make_async_copy(sq_ref.at[:, columns], held.at[g], sems.at[g, len(marks)])
        for k, up_ref in enumerate(up_refs):
            place = ups.at[g, k * rank : (k + 1) * rank, :]
            yield pltpu.make_async_copy(up_ref.at[:, columns], place, sems.at[g, k])

    for g in range(parts):
        for copy in fetches(g):
            copy.start()

    pages_ref[...] = kv_ref[...]

    def owners(rows):
        return rows[:, rank : rank + 1].astype(jnp.float32).astype(jnp.int32)

    def widen(rows, owner, at):
        count = rows.shape[0]
        lanes = lane_iota((count, 2 * rank))
        apart = jnp.bitwise_xor(owner, me)
        twice = jnp.where(lanes < rank, rows, pltpu.roll(rows, rank, 1))
        for k in range(0, len(marks), 2):
            wanted = jnp.where(lanes < rank, marks[k], marks[k + 1])
            kept = jnp.where(apart == wanted, twice, 0.0).astype(jnp.bfloat16)
            wide[at : at + count, k * rank : (k + 2) * rank] = kept

    own_rows, far_rows = own_rows_ref[...], far_rows_ref[...]
    own_owner = owners(own_rows)
    unpack_ref[...] = packing(own_owner, jnp.bitwise_xor(me, PLANE), packed)
    widen(own_rows.astype(jnp.float32), own_owner, 0)
    pack = packing(owners(far_rows), me, packed)
    far_rows = lax.dot_general(pack, far_rows, (((0,), (0,)), ((), ())), preferred_element_type=jnp.float32)
    widen(far_rows, owners(far_rows), tokens)

    for g in range(parts):
        for copy in fetches(g):
            copy.wait()
        columns = slice(g * block, (g + 1) * block)
        result = f32_dot(wide[...], ups[g]).astype(jnp.bfloat16)
        own = result[:tokens].astype(jnp.float32)
        query_ref[:, columns] = (held[g].astype(jnp.float32) + own).astype(jnp.bfloat16)
        far_ref[:, columns] = result[tokens:]


def expand(me, shrunk, far_shrunk, kv, shared_query, ups, packed):
    tokens = shrunk.shape[0]
    marks = tuple(sorted(ups))
    rank, width = ups[0].shape
    block = width // KEY_VALUE_HEADS
    vmem, anywhere = pl.BlockSpec(memory_space=pltpu.VMEM), pl.BlockSpec(memory_space=pl.ANY)
    return pl.pallas_call(
        functools.partial(expand_kernel, marks),
        in_specs=[pl.BlockSpec(memory_space=pltpu.SMEM)] + [vmem] * 3 + [anywhere] * (1 + len(marks)),
        out_specs=[vmem] * 4,
        out_shape=[
            jax.ShapeDtypeStruct(shape, jnp.bfloat16)
            for shape in ((tokens, width), (tokens, packed), kv.shape, (packed, width))
        ],
        scratch_shapes=[
            pltpu.VMEM((tokens + packed, len(marks) * rank), jnp.bfloat16),
            pltpu.VMEM((KEY_VALUE_HEADS, len(marks) * rank, block), jnp.bfloat16),
            pltpu.VMEM((KEY_VALUE_HEADS, tokens, block), jnp.bfloat16),
            pltpu.SemaphoreType.DMA((KEY_VALUE_HEADS, len(marks) + 1)),
        ],
        compiler_params=params(46),
        cost_estimate=cost(16 * tokens * len(marks) * rank * width, 4 * tokens * width),
        name="expand",
    )(me, shrunk, far_shrunk, kv, shared_query, *(ups[k] for k in marks))


def token_kernel(*refs):
    refs[-1][...] = jnp.zeros_like(refs[-1])


def token(*others):
    return pl.pallas_call(
        token_kernel,
        in_specs=[pl.BlockSpec(memory_space=pl.ANY)] * len(others),
        out_specs=pl.BlockSpec(memory_space=pltpu.VMEM),
        out_shape=jax.ShapeDtypeStruct((SUBLANES, 128), jnp.float32),
        compiler_params=params(),
        name="token",
    )(*others)


def hold(rows, *others):
    anywhere = pl.BlockSpec(memory_space=pl.ANY)
    return pl.pallas_call(
        lambda *refs: None,
        in_specs=[anywhere] + [pl.BlockSpec(memory_space=pltpu.HBM)] * len(others),
        out_specs=anywhere,
        out_shape=jax.ShapeDtypeStruct(rows.shape, rows.dtype),
        input_output_aliases={0: 0},
        compiler_params=params(60),
        name="hold",
    )(rows, *others)


def swap_pairs(devices, distance):
    return [(i, i ^ distance) for i in range(devices)]


def mirrored(rows, devices):
    return lax.ppermute(rows, "seq", swap_pairs(devices, devices // 2))


def crossed(factors, devices):
    if lax.axis_size("groups") != 2:
        return mirrored(factors, devices)
    half = factors.shape[1] // 2
    return mirrored(jnp.where(lax.axis_index("groups") == 0, factors[:, :half], factors[:, half:]), devices)


def gathered_factors(factors, here, devices):
    if here.shape != factors.shape:
        first = lax.axis_index("groups") == 0
        there = lax.ppermute(here, "groups", [(0, 1), (1, 0)])
        here = jnp.concatenate([jnp.where(first, here, there), jnp.where(first, there, here)], axis=1)
    held = {0: factors, devices // 2: here}
    bit = devices // 4
    while bit:
        if bit != PLANE:
            swap = swap_pairs(devices, bit)
            held.update({k ^ bit: lax.ppermute(a, "seq", swap) for k, a in list(held.items())})
        bit //= 2
    return held


def window_chunks(kv, devices, reach):
    chunks = [(0, 0, kv)]
    for back in range(1, reach // PLANE + 1):
        hop = back * PLANE
        chunks.append((back, 0, lax.ppermute(kv, "seq", [(i, i + hop) for i in range(devices - hop)])))
    bit = PLANE // 2
    while bit:
        swap = swap_pairs(devices, bit)
        chunks = chunks + [(back, mark ^ bit, lax.ppermute(rows, "seq", swap)) for back, mark, rows in chunks]
        bit //= 2
    return chunks


def attend_kernel(reach, tags, width, me_ref, request_ref, query_ref, unpack_ref, far_ref, *refs):
    chunk_refs, refs = refs[: len(tags)], refs[len(tags) :]
    out_ref, window, keys, values, query, scores, held, far_held, done, sems = refs
    me = me_ref[0]
    parts, tokens, block = held.shape
    heads = block // HEAD_SIZE
    last = len(tags)

    def chunk_fetch(c):
        back, mark = tags[c]
        source = (me // PLANE - back) * PLANE + jnp.bitwise_xor(me % PLANE, mark)
        at = source - me + reach
        place = pl.ds(pl.multiple_of(at * tokens, tokens), tokens)
        copy = pltpu.make_async_copy(chunk_refs[c], window.at[place, :], sems.at[c])
        return (source >= 0) & (at >= 0) & (at <= reach), copy

    def columns(g):
        return pl.ds(pl.multiple_of(g * block, block), block)

    def query_fetches(g):
        return [
            pltpu.make_async_copy(query_ref.at[:, columns(g)], held.at[g], sems.at[last + g]),
            pltpu.make_async_copy(far_ref.at[:, columns(g)], far_held.at[g], sems.at[last + parts + g]),
        ]

    def store(g):
        return pltpu.make_async_copy(done.at[g], out_ref.at[:, columns(g)], sems.at[last + 2 * parts + g])

    for copy in query_fetches(0):
        copy.start()
    for c in range(len(tags)):
        wanted, copy = chunk_fetch(c)
        pl.when(wanted)(copy.start)
    for g in range(1, parts):
        for copy in query_fetches(g):
            copy.start()

    rows, lanes = row_iota((tokens, tokens)), lane_iota((tokens, tokens))
    own = request_ref[pl.ds(me, 1), :].astype(jnp.float32)
    for at in range(reach + 1):
        source = me - reach + at
        span = slice(at * tokens, (at + 1) * tokens)
        theirs = request_ref[pl.ds(jnp.maximum(source, 0), 1), :].astype(jnp.float32)
        theirs = jnp.sum(jnp.where(rows == lanes, theirs, 0.0), axis=1, keepdims=True)
        allowed = jnp.where(source >= 0, theirs, -1.0) == own
        if at == reach:
            allowed = allowed & (rows <= lanes)
        keys[span, HEAD_SIZE:] = jnp.where(allowed, 0.0, -1e30).astype(jnp.bfloat16)

        @pl.when(source < 0)
        def _(span=span):
            window[span, :] = jnp.zeros((tokens, 2 * width), jnp.bfloat16)

    values[:, HEAD_SIZE:] = jnp.ones((values.shape[0], HEAD_SIZE), jnp.bfloat16)
    for j in range(heads):
        query[j, :, HEAD_SIZE:] = (rows == lanes).astype(jnp.bfloat16)
    factor = math.log2(math.e) / math.sqrt(HEAD_SIZE)
    for c in range(len(tags)):
        wanted, copy = chunk_fetch(c)
        pl.when(wanted)(copy.wait)

    @pl.loop(0, parts)
    def _(g):
        for copy in query_fetches(g):
            copy.wait()
        correction = f32_dot(unpack_ref[...], far_held[g])
        corrected = (held[g].astype(jnp.float32) + correction).astype(jnp.bfloat16)
        for j in range(heads):
            query[j, :, 0:HEAD_SIZE] = corrected[:, j * HEAD_SIZE : (j + 1) * HEAD_SIZE]
        at = pl.multiple_of(g * HEAD_SIZE, HEAD_SIZE)
        keys[:, 0:HEAD_SIZE] = window[:, pl.ds(at, HEAD_SIZE)]
        values[:, 0:HEAD_SIZE] = window[:, pl.ds(pl.multiple_of(width + at, HEAD_SIZE), HEAD_SIZE)]

        def score(j):
            stacked = query[4 * j : 4 * j + 4].reshape(4 * tokens, HEAD_SIZE + tokens)
            scores[j % 2] = lax.dot_general(
                stacked, keys[...], (((1,), (1,)), ((), ())), preferred_element_type=jnp.float32
            )

        score(0)
        for j in range(heads // 4):
            if j + 1 < heads // 4:
                score(j + 1)
            for k in range(2):
                masked = scores[j % 2, 2 * k * tokens : 2 * (k + 1) * tokens]
                raised = jnp.exp2((masked - jnp.max(masked, axis=1, keepdims=True)) * factor)
                blended = f32_dot(raised.astype(jnp.bfloat16), values[...])
                for i in range(2):
                    head = 4 * j + 2 * k + i
                    part = blended[i * tokens : (i + 1) * tokens]
                    result = part[:, :HEAD_SIZE] / part[:, HEAD_SIZE:]
                    done[g, :, head * HEAD_SIZE : (head + 1) * HEAD_SIZE] = result.astype(jnp.bfloat16)
        store(g).start()

    for g in range(parts):
        store(g).wait()


def attend(me, requests, query, unpack, far, chunks, reach):
    tokens, query_width = query.shape
    block = query_width // KEY_VALUE_HEADS
    length = (reach + 1) * tokens
    width = chunks[0][2].shape[1] // 2
    vmem, anywhere = pl.BlockSpec(memory_space=pltpu.VMEM), pl.BlockSpec(memory_space=pl.ANY)
    return pl.pallas_call(
        functools.partial(attend_kernel, reach, tuple((b, m) for b, m, _ in chunks), width),
        in_specs=[pl.BlockSpec(memory_space=pltpu.SMEM), vmem, anywhere, vmem] + [anywhere] * (1 + len(chunks)),
        out_specs=anywhere,
        out_shape=jax.ShapeDtypeStruct((tokens, query_width), jnp.bfloat16),
        scratch_shapes=[
            pltpu.VMEM((length, 2 * width), jnp.bfloat16),
            pltpu.VMEM((length, HEAD_SIZE + tokens), jnp.bfloat16),
            pltpu.VMEM((length, 2 * HEAD_SIZE), jnp.bfloat16),
            pltpu.VMEM((block // HEAD_SIZE, tokens, HEAD_SIZE + tokens), jnp.bfloat16),
            pltpu.VMEM((2, 4 * tokens, length), jnp.float32),
            pltpu.VMEM((KEY_VALUE_HEADS, tokens, block), jnp.bfloat16),
            pltpu.VMEM((KEY_VALUE_HEADS, far.shape[0], block), jnp.bfloat16),
            pltpu.VMEM((KEY_VALUE_HEADS, tokens, block), jnp.bfloat16),
            pltpu.SemaphoreType.DMA((len(chunks) + 3 * KEY_VALUE_HEADS,)),
        ],
        compiler_params=params(46),
        cost_estimate=cost(1 * tokens * query_width * length, tokens * query_width),
        name="attend",
    )(me, requests, query, unpack, far, *(rows for _, _, rows in chunks))


def split_kernel(rows_ref, _, left_ref, right_ref):
    width = left_ref.shape[1]
    left_ref[...] = rows_ref[:, :width]
    right_ref[...] = rows_ref[:, width:]


def split(rows, other):
    height, width = rows.shape
    vmem = pl.BlockSpec(memory_space=pltpu.VMEM)
    return pl.pallas_call(
        split_kernel,
        in_specs=[vmem, pl.BlockSpec(memory_space=pl.ANY)],
        out_specs=[vmem, vmem],
        out_shape=[jax.ShapeDtypeStruct((height, width // 2), rows.dtype)] * 2,
        compiler_params=params(),
        name="split",
    )(rows, other)


def exchange(rows, devices):
    width = rows.shape[1]
    out = lax.all_to_all(
        rows.reshape(devices, rows.shape[0] // devices, width), "seq", split_axis=0, concat_axis=0, tiled=True
    )
    return out.reshape(rows.shape)


def local(
    normed,
    shared_query_rows,
    shared_key_rows,
    shared_value_rows,
    token_adapter,
    adapter_slot_table,
    adapter_down_factors,
    adapter_up_query,
    adapter_up_key_value,
    token_request,
):
    tokens = normed.shape[0]
    devices = lax.axis_size("seq")
    reach = devices // 2
    most = max(2, 3 * tokens // (2 * devices))
    fours = -(-most // 4)
    full, fold = fours // 2, fours % 2

    me = lax.axis_index("seq").astype(jnp.int32).reshape(1)
    factors = adapter_up_query[0]
    rank = factors.shape[0]
    here = crossed(factors, devices)
    outgoing, ids = dispatch(normed, token_adapter, adapter_slot_table, full, fold)
    incoming = exchange(hold(outgoing, here), devices)
    ups = gathered_factors(factors, here, devices)
    early = [token(*(ups[k] for k in ups if k))]
    back = exchange(project(incoming, adapter_down_factors, adapter_up_key_value, full, fold, *early), devices)
    kv, shrunk = correct(ids, back, shared_key_rows, shared_value_rows, rank, full, fold)
    swap = swap_pairs(devices, PLANE)
    packed = min(tokens, -(-devices // 2 * most // 16) * 16)
    far_shrunk = lax.ppermute(shrunk, "seq", swap)
    query, unpack, pages, far = expand(me, shrunk, far_shrunk, kv, shared_query_rows, ups, packed)
    chunks = window_chunks(kv, devices, reach)
    pages = exchange(pages, devices)
    far = lax.ppermute(far, "seq", swap)
    requests = token_request.reshape(devices, tokens)
    attention = attend(me, requests, query, unpack, far, chunks, reach)
    return (attention, *split(pages, attention))


def solution(mesh):
    rows = P(("groups", "seq"), None)
    return jax.shard_map(
        local,
        mesh=mesh,
        in_specs=(
            rows,
            rows,
            rows,
            rows,
            rows,
            P(),
            P("seq", None, None),
            P("seq", None, None),
            P("seq", None, None, None),
            P("groups"),
        ),
        out_specs=(rows, rows, rows),
        check_vma=False,
    )
```

```python
import functools
import math

import jax
import jax.numpy as jnp
from jax import lax
from jax.experimental import pallas as pl
from jax.experimental.pallas import tpu as pltpu
from jax.sharding import PartitionSpec as P

KEY_VALUE_HEADS = 4
HEAD_SIZE = 128
SUBLANES = 8
PLANE = 4
MIB = 1024 * 1024


def params(mib=40):
    return pltpu.CompilerParams(vmem_limit_bytes=mib * MIB)


def cost(flops, moved):
    return pl.CostEstimate(flops=flops, bytes_accessed=moved, transcendentals=0)


def f32_dot(a, b):
    return jnp.dot(a, b, preferred_element_type=jnp.float32)


def lane_iota(shape):
    return lax.broadcasted_iota(jnp.int32, shape, 1)


def row_iota(shape):
    return lax.broadcasted_iota(jnp.int32, shape, 0)


def place_tokens(as_row, table_ref, stores):
    count = as_row.shape[1]
    rows, lanes = row_iota((count, count)), lane_iota((count, count))
    adapter = jnp.sum(jnp.where(rows == lanes, as_row, 0.0), axis=1, keepdims=True)
    same = adapter == as_row
    place_col = jnp.sum(jnp.where(same & (lanes < rows), 1.0, 0.0), axis=1, keepdims=True)
    place_row = jnp.sum(jnp.where(same & (rows < lanes), 1.0, 0.0), axis=0, keepdims=True)

    def owner(ids):
        result = jnp.zeros_like(ids)
        for k in range(stores):
            result = jnp.where(ids == float(k), table_ref[k].astype(jnp.float32), result)
        return result

    out = []
    for ids, place in ((adapter, place_col), (as_row, place_row)):
        block = jnp.floor(place * (1.0 / SUBLANES))
        out.append((owner(ids) * SUBLANES + place - block * SUBLANES, block))
    return out


def dispatch_kernel(full, fold, per_width, stores, adapter_ref, table_ref, a_ref, b_ref, x_ref, ids_ref, row_scr):
    step = pl.program_id(0)
    tokens = adapter_ref.shape[1]
    rows = x_ref.shape[0]

    @pl.when(step == 0)
    def _():
        cols, lanes = place_tokens(adapter_ref[...].astype(jnp.float32), table_ref, stores)
        lane = lane_iota((tokens, 128))
        ids_ref[...] = jnp.where(lane == 0, cols[0], jnp.where(lane == 1, cols[1], 0.0)).astype(jnp.int32)
        row_scr[0:1, :] = lanes[0]
        row_scr[1:2, :] = lanes[1]

    at = row_scr[0:1, :].astype(jnp.int32)
    block = row_scr[1:2, :].astype(jnp.int32)
    target = row_iota((rows, tokens))

    if full:

        @pl.when(step < full * per_width)
        def _():
            pick = ((at == target) & (block == step // per_width)).astype(jnp.bfloat16)
            x_ref[...] = f32_dot(pick, a_ref[...]).astype(jnp.bfloat16)

    if fold:

        @pl.when(step >= full * per_width)
        def _():
            low = ((at == target) & (block == full)).astype(jnp.bfloat16)
            high = ((at + 4 == target) & (block == full)).astype(jnp.bfloat16)
            x_ref[...] = (f32_dot(low, a_ref[...]) + f32_dot(high, b_ref[...])).astype(jnp.bfloat16)


def dispatch(normed, token_adapter, table, full, fold):
    tokens, width = normed.shape
    stores = table.shape[0]
    column = width // 4
    per_width, half = width // column, width // 2 // column
    steps = full * per_width + fold * half

    def a_map(i):
        return (0, jnp.where(i < full * per_width, i % per_width, i - full * per_width))

    def b_map(i):
        return (0, jnp.where(i < full * per_width, half, i - full * per_width + half))

    return pl.pallas_call(
        functools.partial(dispatch_kernel, full, fold, per_width, stores),
        grid=(steps,),
        in_specs=[
            pl.BlockSpec((1, tokens), lambda i: (0, 0)),
            pl.BlockSpec(memory_space=pltpu.SMEM),
            pl.BlockSpec((tokens, column), a_map),
            pl.BlockSpec((tokens, column), b_map),
        ],
        out_specs=[
            pl.BlockSpec((stores * SUBLANES, column), lambda i: (0, i)),
            pl.BlockSpec((tokens, 128), lambda i: (0, 0)),
        ],
        out_shape=[
            jax.ShapeDtypeStruct((stores * SUBLANES, steps * column), jnp.bfloat16),
            jax.ShapeDtypeStruct((tokens, 128), jnp.int32),
        ],
        scratch_shapes=[pltpu.VMEM((8, tokens), jnp.float32)],
        compiler_params=params(),
        name="dispatch",
    )(token_adapter.reshape(1, tokens), table, normed, normed)


def project_kernel(full, fold, x_ref, down_ref, up_kv, *refs):
    out_ref = refs[-1]
    rank = up_kv.shape[2]
    width = down_ref.shape[1]
    blocks = [f32_dot(x_ref[:, b * width : (b + 1) * width], down_ref[0]) for b in range(full)]
    if fold:
        rows = x_ref[:, full * width :]
        low, high = f32_dot(rows, down_ref[0, : width // 2]), f32_dot(rows, down_ref[0, width // 2 :])
    kv_width = up_kv.shape[3]
    queries = []
    for b in range(full):
        shrunk = blocks[b].astype(jnp.bfloat16)
        at = b * 2 * kv_width
        for i in range(2):
            piece = shrunk[:, (i + 1) * rank : (i + 2) * rank]
            out_ref[:, at + i * kv_width : at + (i + 1) * kv_width] = f32_dot(piece, up_kv[0, i]).astype(jnp.bfloat16)
        queries.append(shrunk[:, :rank])
    if fold:
        rows = x_ref.shape[0]
        upper = (row_iota((rows, 1)) % SUBLANES) >= 4
        mixed = jnp.where(upper, high, low).reshape(rows // SUBLANES, SUBLANES, 3 * rank)
        both = mixed + jnp.concatenate([mixed[:, 4:], mixed[:, :4]], axis=1)
        shrunk = both.reshape(rows, 3 * rank).astype(jnp.bfloat16)
        delta = [f32_dot(shrunk[:, (i + 1) * rank : (i + 2) * rank], up_kv[0, i]) for i in range(2)]
        at = full * 2 * kv_width
        out_ref[:, at : at + kv_width] = jnp.where(upper, delta[1], delta[0]).astype(jnp.bfloat16)
        queries.append(shrunk[:, :rank])
    if len(queries) % 2:
        queries.append(jnp.zeros_like(queries[0]))
    out_ref[:, (2 * full + fold) * kv_width :] = jnp.concatenate(queries, axis=1)


def project(x, down, up_kv, full, fold, *others):
    rows = x.shape[0]
    _, _, rank, kv_width = up_kv.shape
    shape = (rows, (2 * full + fold) * kv_width + (full + fold + 1) // 2 * 2 * rank)
    vmem = pl.BlockSpec(memory_space=pltpu.VMEM)
    return pl.pallas_call(
        functools.partial(project_kernel, full, fold),
        in_specs=[vmem] * 3 + [pl.BlockSpec(memory_space=pl.ANY)] * len(others),
        out_specs=vmem,
        out_shape=jax.ShapeDtypeStruct(shape, jnp.bfloat16),
        compiler_params=params(),
        name="project",
    )(x, down, up_kv, *others)


def picks(at, chosen, rows):
    return ((at == lane_iota((at.shape[0], rows))) & chosen).astype(jnp.bfloat16)


def correct_kernel(full, fold, rank, ids_ref, back_ref, sk_ref, sv_ref, kv_ref, shrunk_ref):
    rows = back_ref.shape[0]
    width = sk_ref.shape[1]
    place, block = ids_ref[:, 0:1], ids_ref[:, 1:2]
    queries = (2 * full + fold) * width
    total = [0.0, 0.0, 0.0]
    for b in range(full + fold):
        pick = picks(place, block == b, rows)
        for i in range(2):
            if b < full:
                at = (2 * b + i) * width
            else:
                at = 2 * full * width
                pick = pick if i == 0 else picks(place + 4, block == b, rows)
            total[i] += f32_dot(pick, back_ref[:, at : at + width])
    for b in range(full + fold):
        at = queries + b // 2 * 2 * rank
        both = f32_dot(picks(place, block == b, rows), back_ref[:, at : at + 2 * rank])
        total[2] += both if b % 2 == 0 else pltpu.roll(both, rank, 1)
    kv_ref[:, :width] = (sk_ref[...].astype(jnp.float32) + total[0]).astype(jnp.bfloat16)
    kv_ref[:, width:] = (sv_ref[...].astype(jnp.float32) + total[1]).astype(jnp.bfloat16)
    lanes = lane_iota(shrunk_ref.shape)
    owner = (place // SUBLANES).astype(jnp.float32)
    shrunk_ref[...] = jnp.where(lanes < rank, total[2], jnp.where(lanes == rank, owner, 0.0)).astype(jnp.bfloat16)


def correct(ids, back, shared_keys, shared_values, rank, full, fold):
    rows, width = shared_keys.shape
    return pl.pallas_call(
        functools.partial(correct_kernel, full, fold, rank),
        out_shape=[
            jax.ShapeDtypeStruct((rows, 2 * width), jnp.bfloat16),
            jax.ShapeDtypeStruct((rows, 2 * rank), jnp.bfloat16),
        ],
        compiler_params=params(),
        name="correct",
    )(ids, back, shared_keys, shared_values)


def packing(owner, me, rows):
    tokens = owner.shape[0]
    held = jnp.bitwise_and(jnp.bitwise_xor(owner, me), PLANE) == 0
    flags = jnp.broadcast_to(held.astype(jnp.float32), (tokens, tokens)).astype(jnp.bfloat16)
    before = (lane_iota((tokens, tokens)) < row_iota((tokens, tokens))).astype(jnp.bfloat16)
    place = f32_dot(before, flags)[:, :1].astype(jnp.int32)
    return ((place == lane_iota((tokens, rows))) & held).astype(jnp.bfloat16)


def expand_kernel(marks, me_ref, own_rows_ref, far_rows_ref, kv_ref, sq_ref, *refs):
    up_refs, refs = refs[: len(marks)], refs[len(marks) :]
    query_ref, unpack_ref, pages_ref, far_ref, wide, ups, held, sems = refs
    tokens, packed = unpack_ref.shape
    parts, _, block = held.shape
    rank = up_refs[0].shape[0]
    me = me_ref[0]

    def fetches(g):
        columns = slice(g * block, (g + 1) * block)
        yield pltpu.make_async_copy(sq_ref.at[:, columns], held.at[g], sems.at[g, len(marks)])
        for k, up_ref in enumerate(up_refs):
            place = ups.at[g, k * rank : (k + 1) * rank, :]
            yield pltpu.make_async_copy(up_ref.at[:, columns], place, sems.at[g, k])

    for g in range(parts):
        for copy in fetches(g):
            copy.start()

    pages_ref[...] = kv_ref[...]

    def owners(rows):
        return rows[:, rank : rank + 1].astype(jnp.float32).astype(jnp.int32)

    def widen(rows, owner, at):
        count = rows.shape[0]
        lanes = lane_iota((count, 2 * rank))
        apart = jnp.bitwise_xor(owner, me)
        twice = jnp.where(lanes < rank, rows, pltpu.roll(rows, rank, 1))
        for k in range(0, len(marks), 2):
            wanted = jnp.where(lanes < rank, marks[k], marks[k + 1])
            kept = jnp.where(apart == wanted, twice, 0.0).astype(jnp.bfloat16)
            wide[at : at + count, k * rank : (k + 2) * rank] = kept

    own_rows, far_rows = own_rows_ref[...], far_rows_ref[...]
    own_owner = owners(own_rows)
    unpack_ref[...] = packing(own_owner, jnp.bitwise_xor(me, PLANE), packed)
    widen(own_rows.astype(jnp.float32), own_owner, 0)
    pack = packing(owners(far_rows), me, packed)
    far_rows = lax.dot_general(pack, far_rows, (((0,), (0,)), ((), ())), preferred_element_type=jnp.float32)
    widen(far_rows, owners(far_rows), tokens)

    for g in range(parts):
        for copy in fetches(g):
            copy.wait()
        columns = slice(g * block, (g + 1) * block)
        result = f32_dot(wide[...], ups[g]).astype(jnp.bfloat16)
        own = result[:tokens].astype(jnp.float32)
        query_ref[:, columns] = (held[g].astype(jnp.float32) + own).astype(jnp.bfloat16)
        far_ref[:, columns] = result[tokens:]


def expand(me, shrunk, far_shrunk, kv, shared_query, ups, packed):
    tokens = shrunk.shape[0]
    marks = tuple(sorted(ups))
    rank, width = ups[0].shape
    block = width // KEY_VALUE_HEADS
    vmem, anywhere = pl.BlockSpec(memory_space=pltpu.VMEM), pl.BlockSpec(memory_space=pl.ANY)
    return pl.pallas_call(
        functools.partial(expand_kernel, marks),
        in_specs=[pl.BlockSpec(memory_space=pltpu.SMEM)] + [vmem] * 3 + [anywhere] * (1 + len(marks)),
        out_specs=[vmem] * 4,
        out_shape=[
            jax.ShapeDtypeStruct(shape, jnp.bfloat16)
            for shape in ((tokens, width), (tokens, packed), kv.shape, (packed, width))
        ],
        scratch_shapes=[
            pltpu.VMEM((tokens + packed, len(marks) * rank), jnp.bfloat16),
            pltpu.VMEM((KEY_VALUE_HEADS, len(marks) * rank, block), jnp.bfloat16),
            pltpu.VMEM((KEY_VALUE_HEADS, tokens, block), jnp.bfloat16),
            pltpu.SemaphoreType.DMA((KEY_VALUE_HEADS, len(marks) + 1)),
        ],
        compiler_params=params(46),
        cost_estimate=cost(16 * tokens * len(marks) * rank * width, 4 * tokens * width),
        name="expand",
    )(me, shrunk, far_shrunk, kv, shared_query, *(ups[k] for k in marks))


def token_kernel(*refs):
    refs[-1][...] = jnp.zeros_like(refs[-1])


def token(*others):
    return pl.pallas_call(
        token_kernel,
        in_specs=[pl.BlockSpec(memory_space=pl.ANY)] * len(others),
        out_specs=pl.BlockSpec(memory_space=pltpu.VMEM),
        out_shape=jax.ShapeDtypeStruct((SUBLANES, 128), jnp.float32),
        compiler_params=params(),
        name="token",
    )(*others)


def hold(rows, *others):
    anywhere = pl.BlockSpec(memory_space=pl.ANY)
    return pl.pallas_call(
        lambda *refs: None,
        in_specs=[anywhere] + [pl.BlockSpec(memory_space=pltpu.HBM)] * len(others),
        out_specs=anywhere,
        out_shape=jax.ShapeDtypeStruct(rows.shape, rows.dtype),
        input_output_aliases={0: 0},
        compiler_params=params(60),
        name="hold",
    )(rows, *others)


def swap_pairs(devices, distance):
    return [(i, i ^ distance) for i in range(devices)]


def mirrored(rows, devices):
    return lax.ppermute(rows, "seq", swap_pairs(devices, devices // 2))


def crossed(factors, devices):
    if lax.axis_size("groups") != 2:
        return mirrored(factors, devices)
    half = factors.shape[1] // 2
    return mirrored(jnp.where(lax.axis_index("groups") == 0, factors[:, :half], factors[:, half:]), devices)


def gathered_factors(factors, here, devices):
    if here.shape != factors.shape:
        first = lax.axis_index("groups") == 0
        there = lax.ppermute(here, "groups", [(0, 1), (1, 0)])
        here = jnp.concatenate([jnp.where(first, here, there), jnp.where(first, there, here)], axis=1)
    held = {0: factors, devices // 2: here}
    bit = devices // 4
    while bit:
        if bit != PLANE:
            swap = swap_pairs(devices, bit)
            held.update({k ^ bit: lax.ppermute(a, "seq", swap) for k, a in list(held.items())})
        bit //= 2
    return held


def window_chunks(kv, devices, reach):
    chunks = [(0, 0, kv)]
    for back in range(reach // PLANE, 0, -1):
        hop = back * PLANE
        chunks.append((back, 0, lax.ppermute(kv, "seq", [(i, i + hop) for i in range(devices - hop)])))
    bit = PLANE // 2
    while bit:
        swap = swap_pairs(devices, bit)
        chunks = chunks + [(back, mark ^ bit, lax.ppermute(rows, "seq", swap)) for back, mark, rows in chunks]
        bit //= 2
    return chunks


def attend_kernel(reach, tags, width, me_ref, request_ref, query_ref, unpack_ref, far_ref, *refs):
    chunk_refs, refs = refs[: len(tags)], refs[len(tags) :]
    out_ref, window, keys, values, query, scores, held, far_held, done, sems = refs
    me = me_ref[0]
    parts, tokens, block = held.shape
    heads = block // HEAD_SIZE
    last = len(tags)

    def chunk_fetch(c):
        back, mark = tags[c]
        source = (me // PLANE - back) * PLANE + jnp.bitwise_xor(me % PLANE, mark)
        at = source - me + reach
        place = pl.ds(pl.multiple_of(at * tokens, tokens), tokens)
        copy = pltpu.make_async_copy(chunk_refs[c], window.at[place, :], sems.at[c])
        return (source >= 0) & (at >= 0) & (at <= reach), copy

    def columns(g):
        return pl.ds(pl.multiple_of(g * block, block), block)

    def query_fetches(g):
        return [
            pltpu.make_async_copy(query_ref.at[:, columns(g)], held.at[g], sems.at[last + g]),
            pltpu.make_async_copy(far_ref.at[:, columns(g)], far_held.at[g], sems.at[last + parts + g]),
        ]

    def store(g):
        return pltpu.make_async_copy(done.at[g], out_ref.at[:, columns(g)], sems.at[last + 2 * parts + g])

    for copy in query_fetches(0):
        copy.start()
    for c in range(len(tags)):
        wanted, copy = chunk_fetch(c)
        pl.when(wanted)(copy.start)
    for g in range(1, parts):
        for copy in query_fetches(g):
            copy.start()

    rows, lanes = row_iota((tokens, tokens)), lane_iota((tokens, tokens))
    own = request_ref[pl.ds(me, 1), :].astype(jnp.float32)
    for at in range(reach + 1):
        source = me - reach + at
        span = slice(at * tokens, (at + 1) * tokens)
        theirs = request_ref[pl.ds(jnp.maximum(source, 0), 1), :].astype(jnp.float32)
        theirs = jnp.sum(jnp.where(rows == lanes, theirs, 0.0), axis=1, keepdims=True)
        allowed = jnp.where(source >= 0, theirs, -1.0) == own
        if at == reach:
            allowed = allowed & (rows <= lanes)
        keys[span, HEAD_SIZE:] = jnp.where(allowed, 0.0, -1e30).astype(jnp.bfloat16)

        @pl.when(source < 0)
        def _(span=span):
            window[span, :] = jnp.zeros((tokens, 2 * width), jnp.bfloat16)

    values[:, HEAD_SIZE:] = jnp.ones((values.shape[0], HEAD_SIZE), jnp.bfloat16)
    for j in range(heads):
        query[j, :, HEAD_SIZE:] = (rows == lanes).astype(jnp.bfloat16)
    factor = math.log2(math.e) / math.sqrt(HEAD_SIZE)
    for c in range(len(tags)):
        wanted, copy = chunk_fetch(c)
        pl.when(wanted)(copy.wait)

    @pl.loop(0, parts)
    def _(g):
        for copy in query_fetches(g):
            copy.wait()
        correction = f32_dot(unpack_ref[...], far_held[g])
        corrected = (held[g].astype(jnp.float32) + correction).astype(jnp.bfloat16)
        for j in range(heads):
            query[j, :, 0:HEAD_SIZE] = corrected[:, j * HEAD_SIZE : (j + 1) * HEAD_SIZE]
        at = pl.multiple_of(g * HEAD_SIZE, HEAD_SIZE)
        keys[:, 0:HEAD_SIZE] = window[:, pl.ds(at, HEAD_SIZE)]
        values[:, 0:HEAD_SIZE] = window[:, pl.ds(pl.multiple_of(width + at, HEAD_SIZE), HEAD_SIZE)]

        def score(j):
            stacked = query[4 * j : 4 * j + 4].reshape(4 * tokens, HEAD_SIZE + tokens)
            scores[j % 2] = lax.dot_general(
                stacked, keys[...], (((1,), (1,)), ((), ())), preferred_element_type=jnp.float32
            )

        score(0)
        for j in range(heads // 4):
            if j + 1 < heads // 4:
                score(j + 1)
            for k in range(2):
                masked = scores[j % 2, 2 * k * tokens : 2 * (k + 1) * tokens]
                raised = jnp.exp2((masked - jnp.max(masked, axis=1, keepdims=True)) * factor)
                blended = f32_dot(raised.astype(jnp.bfloat16), values[...])
                for i in range(2):
                    head = 4 * j + 2 * k + i
                    part = blended[i * tokens : (i + 1) * tokens]
                    result = part[:, :HEAD_SIZE] / part[:, HEAD_SIZE:]
                    done[g, :, head * HEAD_SIZE : (head + 1) * HEAD_SIZE] = result.astype(jnp.bfloat16)
        store(g).start()

    for g in range(parts):
        store(g).wait()


def attend(me, requests, query, unpack, far, chunks, reach):
    tokens, query_width = query.shape
    block = query_width // KEY_VALUE_HEADS
    length = (reach + 1) * tokens
    width = chunks[0][2].shape[1] // 2
    vmem, anywhere = pl.BlockSpec(memory_space=pltpu.VMEM), pl.BlockSpec(memory_space=pl.ANY)
    return pl.pallas_call(
        functools.partial(attend_kernel, reach, tuple((b, m) for b, m, _ in chunks), width),
        in_specs=[pl.BlockSpec(memory_space=pltpu.SMEM), vmem, anywhere, vmem] + [anywhere] * (1 + len(chunks)),
        out_specs=anywhere,
        out_shape=jax.ShapeDtypeStruct((tokens, query_width), jnp.bfloat16),
        scratch_shapes=[
            pltpu.VMEM((length, 2 * width), jnp.bfloat16),
            pltpu.VMEM((length, HEAD_SIZE + tokens), jnp.bfloat16),
            pltpu.VMEM((length, 2 * HEAD_SIZE), jnp.bfloat16),
            pltpu.VMEM((block // HEAD_SIZE, tokens, HEAD_SIZE + tokens), jnp.bfloat16),
            pltpu.VMEM((2, 4 * tokens, length), jnp.float32),
            pltpu.VMEM((KEY_VALUE_HEADS, tokens, block), jnp.bfloat16),
            pltpu.VMEM((KEY_VALUE_HEADS, far.shape[0], block), jnp.bfloat16),
            pltpu.VMEM((KEY_VALUE_HEADS, tokens, block), jnp.bfloat16),
            pltpu.SemaphoreType.DMA((len(chunks) + 3 * KEY_VALUE_HEADS,)),
        ],
        compiler_params=params(46),
        cost_estimate=cost(1 * tokens * query_width * length, tokens * query_width),
        name="attend",
    )(me, requests, query, unpack, far, *(rows for _, _, rows in chunks))


def split_kernel(rows_ref, _, left_ref, right_ref):
    width = left_ref.shape[1]
    left_ref[...] = rows_ref[:, :width]
    right_ref[...] = rows_ref[:, width:]


def split(rows, other):
    height, width = rows.shape
    vmem = pl.BlockSpec(memory_space=pltpu.VMEM)
    return pl.pallas_call(
        split_kernel,
        in_specs=[vmem, pl.BlockSpec(memory_space=pl.ANY)],
        out_specs=[vmem, vmem],
        out_shape=[jax.ShapeDtypeStruct((height, width // 2), rows.dtype)] * 2,
        compiler_params=params(),
        name="split",
    )(rows, other)


def exchange(rows, devices):
    width = rows.shape[1]
    out = lax.all_to_all(
        rows.reshape(devices, rows.shape[0] // devices, width), "seq", split_axis=0, concat_axis=0, tiled=True
    )
    return out.reshape(rows.shape)


def local(
    normed,
    shared_query_rows,
    shared_key_rows,
    shared_value_rows,
    token_adapter,
    adapter_slot_table,
    adapter_down_factors,
    adapter_up_query,
    adapter_up_key_value,
    token_request,
):
    tokens = normed.shape[0]
    devices = lax.axis_size("seq")
    reach = devices // 2
    most = max(2, 3 * tokens // (2 * devices))
    fours = -(-most // 4)
    full, fold = fours // 2, fours % 2

    me = lax.axis_index("seq").astype(jnp.int32).reshape(1)
    factors = adapter_up_query[0]
    rank = factors.shape[0]
    here = crossed(factors, devices)
    outgoing, ids = dispatch(normed, token_adapter, adapter_slot_table, full, fold)
    incoming = exchange(hold(outgoing, here), devices)
    ups = gathered_factors(factors, here, devices)
    early = [token(*(ups[k] for k in ups if k))]
    back = exchange(project(incoming, adapter_down_factors, adapter_up_key_value, full, fold, *early), devices)
    kv, shrunk = correct(ids, back, shared_key_rows, shared_value_rows, rank, full, fold)
    swap = swap_pairs(devices, PLANE)
    packed = min(tokens, -(-devices // 2 * most // 16) * 16)
    far_shrunk = lax.ppermute(shrunk, "seq", swap)
    query, unpack, pages, far = expand(me, shrunk, far_shrunk, kv, shared_query_rows, ups, packed)
    chunks = window_chunks(kv, devices, reach)
    pages = exchange(pages, devices)
    far = lax.ppermute(far, "seq", swap)
    requests = token_request.reshape(devices, tokens)
    attention = attend(me, requests, query, unpack, far, chunks, reach)
    return (attention, *split(pages, attention))


def solution(mesh):
    rows = P(("groups", "seq"), None)
    return jax.shard_map(
        local,
        mesh=mesh,
        in_specs=(
            rows,
            rows,
            rows,
            rows,
            rows,
            P(),
            P("seq", None, None),
            P("seq", None, None),
            P("seq", None, None, None),
            P("groups"),
        ),
        out_specs=(rows, rows, rows),
        check_vma=False,
    )
```
